32 devices in a mesh: row: 4 (over z), col: 8 (over y, x, core).
Axes of the slice: x: 2, y: 2, z: 4, core: 2. Of those that a mesh axis runs over, the one named last changes fastest.
Arguments:
- spectra: bfloat16 [6144, 144, 128], P(('row', 'col')), may hold values from -30 to 30
- station_ids: int32 [6144], P(('row', 'col')), may hold values from 0 to 3071, as said below
- counts: int32 [32], P(('row', 'col')), may hold values from 0 to 192, as said below
Outputs:
- cross_spectra: bfloat16 [3, 2, 3072, 3072], P(None, None, 'row', 'col')
The draws below stay inside these ranges and needn't reach their ends.
Inputs may be any that keep to these rules, and one draw needn't show every extreme that they name: `station_ids`: the live slots of all readers name every station exactly once; slots at or past a reader's count hold arbitrary station numbers and carry no data. The counts sum to 3072. Among the live slots of one reader, at most 6 name stations of one block h * 96 to h * 96 + 95, and that number is reached in every draw.
All inputs are finite; a program needn't handle non-finite values.
Results may differ from the reference program's by a relative error of at most 0.001.
Values may be sent and summed in bfloat16 or wider, within the bound.
No kernel may reach another device: no remote copies, remote signals or barrier semaphores. Data moves between devices by JAX's collectives and lax.ppermute only.
A program may use at most 128 MiB of HBM per device.

```python
import math
import jax
import jax.numpy as jnp
from jax import lax

SD = 96
SEG = 144
NB = 64
READERS = 32
CAP = 192
STATIONS = 3072
N_ROW = 4
N_COL = 8


def layout_plan(key):
    base_key = jax.random.fold_in(key, 17)
    subkeys = jax.random.split(base_key, 5)
    pair_count = READERS // 2
    merged = jax.random.randint(subkeys[0], (pair_count,), 0, 2)
    forced = jax.random.randint(subkeys[1], (), 0, pair_count)
    merged = jnp.where(jnp.arange(pair_count) == forced, 1, merged)
    receiver_side = jax.random.randint(subkeys[2], (pair_count,), 0, 2)
    station = jnp.arange(STATIONS, dtype=jnp.int32)
    within_block = station % SD
    reader_of = (station // SD + within_block // 2 + within_block % 2 * (READERS // 2)) % READERS
    pair_index = reader_of // 2
    reader_of = jnp.where(merged[pair_index] == 1, 2 * pair_index + receiver_side[pair_index], reader_of)
    counts = jax.ops.segment_sum(jnp.ones_like(station), reader_of, num_segments=READERS)
    shuffle = jax.random.permutation(subkeys[3], STATIONS).astype(jnp.int32)
    ordered = jnp.argsort(reader_of * STATIONS + shuffle, stable=True).astype(jnp.int32)
    offsets = jnp.cumsum(counts) - counts
    slot_index = jnp.arange(CAP, dtype=jnp.int32)
    position = offsets[:, None] + slot_index[None, :]
    is_live = slot_index[None, :] < counts[:, None]
    filler = jax.random.randint(subkeys[4], (READERS, CAP), 0, STATIONS)
    station_list = jnp.where(is_live, ordered[jnp.clip(position, 0, STATIONS - 1)], filler)
    return (station_list.reshape(-1).astype(jnp.int32), counts.astype(jnp.int32))


def draw_station_ids(key, part):
    return layout_plan(key)[0]


def draw_counts(key, part):
    return layout_plan(key)[1]


def draw_spectra(key, part):
    subkeys = jax.random.split(jax.random.fold_in(key, 29), 3)
    full_shape = (READERS * CAP, SEG, 2 * NB)
    row_scale = jnp.exp(jax.random.uniform(subkeys[0], (READERS * CAP, SEG, 1), jnp.float32, math.log(0.3), math.log(3.0)))
    bin_scale = jnp.exp(jax.random.uniform(subkeys[1], (READERS * CAP, SEG, NB), jnp.float32, math.log(0.5), math.log(2.0)))
    bin_scale = jnp.concatenate([bin_scale, bin_scale], axis=2)
    noise = jnp.clip(jax.random.normal(subkeys[2], full_shape, jnp.float32), -4.0, 4.0)
    return (noise * row_scale * bin_scale).astype(jnp.bfloat16)


def setup_inputs(seed: int = 0) -> dict:
    arg_keys = jax.random.split(jax.random.key(seed), 4)
    spectra = draw_spectra(jax.random.fold_in(arg_keys[3], 71), 0)
    station_ids = draw_station_ids(jax.random.fold_in(arg_keys[3], 71), 0)
    counts = draw_counts(jax.random.fold_in(arg_keys[3], 71), 0)
    return dict(spectra=spectra, station_ids=station_ids, counts=counts)


power_floor = 0.25

def whiten(raw):
    values = raw.astype(jnp.float32)
    band = values.shape[2] // 2
    real_part = values[:, :, :band]
    imag_part = values[:, :, band:]
    energy = real_part * real_part + imag_part * imag_part
    pieces = []
    for bin_index in range(3):
        lower = bin_index * band // 4
        averaged = lax.optimization_barrier(jnp.mean(energy[:, :, lower:lower + band // 2], axis=2))
        amplitude = jnp.sqrt(jnp.maximum(averaged, power_floor))
        center = lower + band // 4
        pieces.append(real_part[:, :, center] / amplitude)
        pieces.append(imag_part[:, :, center] / amplitude)
    return jnp.concatenate(pieces, axis=1)

def reference(spectra, station_ids, counts):
    blocks = spectra.reshape(READERS, CAP, SEG, 2 * NB)
    id_blocks = station_ids.reshape(READERS, CAP)
    slot_index = jnp.arange(CAP, dtype=jnp.int32)

    def absorb(white, inputs):
        raw, station_list, live_count = inputs
        whitened = whiten(raw)
        target = jnp.where(slot_index < live_count, station_list, STATIONS).astype(jnp.int32)
        return (white.at[target].set(whitened, mode='drop'), None)
    start = jnp.zeros((STATIONS, 6 * SEG), jnp.float32)
    white, unused = lax.scan(absorb, start, (blocks, id_blocks, counts))
    column = jnp.arange(STATIONS, dtype=jnp.int32)
    sigma = (column // SD % N_ROW * N_COL + column // (SD * N_ROW)) * SD + column % SD
    column_white = white[sigma]
    norm_factor = 1.0 / math.sqrt(SEG)
    row_block = STATIONS // N_ROW
    outputs = []
    for bin_index in range(3):
        real_imag = white[:, bin_index * 2 * SEG:(bin_index + 1) * 2 * SEG]
        rotated = jnp.concatenate([real_imag[:, SEG:], -real_imag[:, :SEG]], axis=1)
        other = column_white[:, bin_index * 2 * SEG:(bin_index + 1) * 2 * SEG]

        def tile_rows(pair):
            stacked = jnp.concatenate([pair[0], pair[1]], axis=0)
            product = lax.dot_general(stacked, other, (((1,), (1,)), ((), ())), precision=lax.Precision.HIGHEST, preferred_element_type=jnp.float32)
            return (product * norm_factor).astype(jnp.bfloat16).reshape(2, row_block, STATIONS)
        tiles = lax.map(tile_rows, (real_imag.reshape(N_ROW, row_block, 2 * SEG), rotated.reshape(N_ROW, row_block, 2 * SEG)))
        outputs.append(jnp.transpose(tiles, (1, 0, 2, 3)).reshape(2, STATIONS, STATIONS))
    return jnp.stack(outputs, axis=0)
```

```python
import functools
import math

import jax
import jax.numpy as jnp
from jax import lax
from jax.experimental import pallas as pl
from jax.experimental.pallas import tpu as pltpu
from jax.sharding import PartitionSpec as P

power_floor = 0.25
bins = 3
lanes = 128
group = 8
slab = 8
full = 32767.0
vmem_bytes = 48 * 1024 * 1024

tail_tile = 2 * bins
width = (tail_tile + 1) * lanes


def meta_lane(segments):
    return tail_tile * (segments - lanes)


def dot_t(a, b):
    return lax.dot_general(a, b, (((1,), (1,)), ((), ())), preferred_element_type=jnp.float32)


def split(q):
    high = jnp.floor((q + 128.0) * (1.0 / 256.0))
    return (high * 256.0).astype(jnp.bfloat16), (q - high * 256.0).astype(jnp.bfloat16)


def iota(shape, dim):
    return lax.broadcasted_iota(jnp.int32, shape, dim)


def whiten_kernel(home_rows, count_ref, ids_ref, x_ref, out_ref, sel_ref, win_ref, id_ref, coded_ref):
    step = pl.program_id(0)
    slots_step, segments, two_band = x_ref.shape
    band = two_band // 2
    tail = segments - lanes
    slot_count = ids_ref.shape[1]
    rows = 2 * bins * group

    @pl.when(step == 0)
    def _():
        row = iota((rows, group * two_band), 0)
        col = iota((rows, group * two_band), 1)
        part = row // group
        same = (row % group) == (col // two_band)
        lane = col % two_band
        lower = (part // 2) * (band // 4)
        center = (part % 2) * band + lower + band // 4
        one = jnp.float32(1.0)
        sel_ref[...] = jnp.where(same & (lane == center), one, 0.0).astype(jnp.bfloat16)
        within = lane % band
        inside = (within >= lower) & (within < lower + band // 2)
        win_ref[...] = jnp.where(same & inside, one, 0.0).astype(jnp.bfloat16)
        ids = ids_ref[...].astype(jnp.float32)
        local = ids - home_rows * jnp.floor((ids + 0.5) * (1.0 / home_rows))
        eye = iota((slot_count, slot_count), 0) == iota((slot_count, slot_count), 1)
        id_ref[...] = jnp.sum(jnp.where(eye, local + 1.0, 0.0), axis=1, keepdims=True)

    def body(g, carry):
        x = x_ref[pl.ds(g * group, group)]
        xs = jnp.concatenate([x[s] for s in range(group)], axis=1)
        xf = xs.astype(jnp.float32)
        energy = xf * xf
        high = energy.astype(jnp.bfloat16)
        low = (energy - high.astype(jnp.float32)).astype(jnp.bfloat16)
        picked = dot_t(sel_ref[...], xs)
        total = dot_t(win_ref[...], high) + dot_t(win_ref[...], low)
        white = picked / jnp.sqrt(jnp.maximum(total * (2.0 / band), power_floor))
        first = pl.multiple_of(step * slots_step + g * group, group)
        coded = []
        expos = []
        mants = []
        for f in range(bins):
            pair = white[2 * f * group : 2 * (f + 1) * group]
            size = jnp.maximum(jnp.abs(pair[:group]), jnp.abs(pair[group:]))
            peak = jnp.maximum(jnp.max(size, axis=1, keepdims=True), 1e-30)
            expo = jnp.ceil(jnp.log2(peak))
            mant = jnp.floor(peak * jnp.exp2(-expo) * 16384.0) + 1.0
            inverse = (full * 16384.0) / (mant * jnp.exp2(expo))
            expos.append(expo)
            mants.append(mant)
            for p in range(2):
                q = jnp.round(pair[p * group : (p + 1) * group] * inverse)
                coded.append(jnp.clip(q, -full, full))
        for t in range(tail_tile):
            coded_ref[pl.ds(first, group), t * lanes : (t + 1) * lanes] = coded[t][:, :lanes]
        last = [c[:, lanes:] for c in coded] + mants + expos + [id_ref[pl.ds(first, group), :]]
        used = tail_tile * tail + 2 * bins + 1
        last.append(jnp.zeros((group, lanes - used), jnp.float32))
        coded_ref[pl.ds(first, group), tail_tile * lanes :] = jnp.concatenate(last, axis=1)
        return carry

    lax.fori_loop(0, slots_step // group, body, 0)

    @pl.when(step == pl.num_programs(0) - 1)
    def _():
        ids = ids_ref[...].astype(jnp.float32)
        target = jnp.floor((ids + 0.5) * (1.0 / home_rows))
        shape = (slot_count, slot_count)
        j = iota(shape, 0)
        i = iota(shape, 1)
        target_column = jnp.sum(jnp.where(j == i, target, 0.0), axis=1, keepdims=True)
        count = count_ref[0]
        ahead = (j < i) & (j < count) & (target_column == target)
        within = jnp.sum(jnp.where(ahead, 1.0, 0.0), axis=0, keepdims=True)
        live = iota((1, slot_count), 1) < count
        place = jnp.where(live, target * slab + within, -1.0)
        send_rows = out_ref.shape[0]
        spot = iota((send_rows, slot_count), 0).astype(jnp.float32)
        chosen = jnp.where(spot == place, 1.0, 0.0).astype(jnp.bfloat16)
        high, low = split(coded_ref[...])
        sent = jnp.dot(chosen, high, preferred_element_type=jnp.float32)
        sent += jnp.dot(chosen, low, preferred_element_type=jnp.float32)
        out_ref[...] = sent.astype(jnp.int32).astype(jnp.int16)


def whiten_pack(spectra, station_ids, counts, readers):
    slot_count, segments, two_band = spectra.shape
    home_rows = slot_count // 2
    slots_step = 32
    rows = 2 * bins * group
    return pl.pallas_call(
        functools.partial(whiten_kernel, home_rows),
        grid=(slot_count // slots_step,),
        out_shape=jax.ShapeDtypeStruct((readers * slab, width), jnp.int16),
        in_specs=[
            pl.BlockSpec(memory_space=pltpu.SMEM),
            pl.BlockSpec((1, slot_count), lambda i: (0, 0)),
            pl.BlockSpec((slots_step, segments, two_band), lambda i: (i, 0, 0)),
        ],
        out_specs=pl.BlockSpec((readers * slab, width), lambda i: (0, 0)),
        scratch_shapes=[
            pltpu.VMEM((rows, group * two_band), jnp.bfloat16),
            pltpu.VMEM((rows, group * two_band), jnp.bfloat16),
            pltpu.VMEM((slot_count, 1), jnp.float32),
            pltpu.VMEM((slot_count, width), jnp.float32),
        ],
        compiler_params=pltpu.CompilerParams(vmem_limit_bytes=vmem_bytes),
        name="whiten_pack",
    )(counts, station_ids.reshape(1, slot_count), spectra)


def settle_kernel(id_lane, in_ref, out_ref):
    home_rows = out_ref.shape[0]
    q = in_ref[...].astype(jnp.int32).astype(jnp.float32)
    station = q[:, id_lane : id_lane + 1]
    wanted = (iota((q.shape[0], home_rows), 1) + 1).astype(jnp.float32)
    chosen = jnp.where(station == wanted, 1.0, 0.0).astype(jnp.bfloat16)
    high, low = split(q)
    dims = (((0,), (0,)), ((), ()))
    home = lax.dot_general(chosen, high, dims, preferred_element_type=jnp.float32)
    home += lax.dot_general(chosen, low, dims, preferred_element_type=jnp.float32)
    out_ref[...] = home.astype(jnp.int32).astype(jnp.int16)


def settle(received, home_rows, segments):
    id_lane = tail_tile * lanes + meta_lane(segments) + 2 * bins
    return pl.pallas_call(
        functools.partial(settle_kernel, id_lane),
        out_shape=jax.ShapeDtypeStruct((home_rows, width), jnp.int16),
        compiler_params=pltpu.CompilerParams(vmem_limit_bytes=vmem_bytes),
        name="settle",
    )(received)


def roll(x, shift):
    return pltpu.roll(x, shift % x.shape[1], 1)


def pair_kernel(segments, row_n, col_n, place_ref, *refs):
    row_refs = refs[:row_n]
    col_refs = refs[row_n : row_n + col_n]
    out_ref, a_ref, b_ref, scale_ref, tail_ref = refs[row_n + col_n :]
    f = pl.program_id(0)
    home_rows = row_refs[0].shape[0]
    tail = segments - lanes
    meta = meta_lane(segments)
    columns = col_n * home_rows
    lane = iota((home_rows, lanes), 1)
    unit = 1.0 / (16384.0 * full)

    def load(ref):
        start = pl.multiple_of(f * 2 * lanes, 2 * lanes)
        main = ref[:, pl.ds(start, 2 * lanes)].astype(jnp.int32).astype(jnp.float32)
        last = ref[:, tail_tile * lanes :].astype(jnp.int32).astype(jnp.float32)
        mine = pltpu.roll(last, lax.rem(lanes - f * 2 * tail, lanes), 1)
        return main, last, jnp.where(lane < 2 * tail, mine, 0.0)

    def ends(first, second, third):
        return first + roll(second, 2 * tail) + roll(third, 4 * tail)

    def wide(x):
        return x[0].astype(jnp.float32), x[1].astype(jnp.float32)

    for k in range(row_n):
        main, last, mine = load(row_refs[k])
        start = pl.multiple_of(place_ref[0, k] * home_rows, home_rows)
        high, low = split(main)
        tail_high, tail_low = wide(split(mine))
        ending = ends(tail_high, tail_low, tail_high).astype(jnp.bfloat16)
        a_ref[pl.ds(start, home_rows), :] = jnp.concatenate([high, low, high, ending], axis=1)
        power = last * jnp.exp2(roll(last, -bins))
        scale = jnp.sum(jnp.where(lane == meta + f, power, 0.0), axis=1, keepdims=True)
        scale_ref[pl.ds(start, home_rows), :] = scale * unit

    for k in range(col_n):
        main, last, mine = load(col_refs[k])
        turned = jnp.concatenate([-main[:, lanes:], main[:, :lanes]], axis=1)
        mine_turned = jnp.where(lane < tail, -roll(mine, -tail), roll(mine, tail))
        mine_turned = jnp.where(lane < 2 * tail, mine_turned, 0.0)
        start = pl.multiple_of(place_ref[1, k] * home_rows, home_rows)
        for offset, value, end in ((0, main, mine), (columns, turned, mine_turned)):
            high, low = split(value)
            tail_high, tail_low = wide(split(end))
            ending = ends(tail_high, tail_high, tail_low).astype(jnp.bfloat16)
            b_ref[pl.ds(offset + start, home_rows), :] = jnp.concatenate([high, high, low, ending], axis=1)
        tail_ref[pl.ds(start, home_rows), :] = last

    pick = iota((8, lanes), 0)
    want = jnp.where(pick == 0, meta + f, meta + bins + f)
    chosen = jnp.where((iota((8, lanes), 1) == want) & (pick < 2), 1.0, 0.0).astype(jnp.bfloat16)
    high, low = split(tail_ref[...])
    codes = dot_t(chosen, high) + dot_t(chosen, low)
    column_scale = codes[0:1] * jnp.exp2(codes[1:2]) * (unit / math.sqrt(segments))

    product = dot_t(a_ref[...], b_ref[...])
    row_scale = scale_ref[...]
    for p in range(2):
        value = product[:, p * columns : (p + 1) * columns] * row_scale * column_scale
        out_ref[0, p] = value.astype(jnp.bfloat16)


def pair_tiles(row_blocks, row_index, col_blocks, col_index, segments):
    row_n, col_n = len(row_blocks), len(col_blocks)
    home_rows = row_blocks[0].shape[0]
    rows, columns = row_n * home_rows, col_n * home_rows
    most = max(row_n, col_n)
    place = jnp.stack([
        jnp.pad(row_index, (0, most - row_n)),
        jnp.pad(col_index, (0, most - col_n)),
    ])
    block = pl.BlockSpec((home_rows, width), lambda f, place: (0, 0))
    depth = 7 * lanes
    return pl.pallas_call(
        functools.partial(pair_kernel, segments, row_n, col_n),
        grid_spec=pltpu.PrefetchScalarGridSpec(
            num_scalar_prefetch=1,
            grid=(bins,),
            in_specs=[block] * (row_n + col_n),
            out_specs=pl.BlockSpec((1, 2, rows, columns), lambda f, place: (f, 0, 0, 0)),
            scratch_shapes=[
                pltpu.VMEM((rows, depth), jnp.bfloat16),
                pltpu.VMEM((2 * columns, depth), jnp.bfloat16),
                pltpu.VMEM((rows, 1), jnp.float32),
                pltpu.VMEM((columns, lanes), jnp.float32),
            ],
        ),
        out_shape=jax.ShapeDtypeStruct((bins, 2, rows, columns), jnp.bfloat16),
        compiler_params=pltpu.CompilerParams(vmem_limit_bytes=vmem_bytes),
        name="pair_tiles",
    )(place, *row_blocks, *col_blocks)


def across(value, axis, distance):
    size = lax.axis_size(axis)
    return lax.ppermute(value, axis, [(i, i ^ distance) for i in range(size)])


def shards(spectra, station_ids, counts):
    row_count = lax.axis_size("row")
    column_count = lax.axis_size("col")
    readers = row_count * column_count
    slot_count, segments, _ = spectra.shape
    home_rows = slot_count // 2
    packed = whiten_pack(spectra, station_ids, counts, readers)
    received = lax.all_to_all(packed, ("row", "col"), split_axis=0, concat_axis=0, tiled=True)
    white = settle(received, home_rows, segments)
    row_blocks = [None] * column_count
    row_blocks[0] = white
    col_blocks = [white]
    for k in range(1, row_count):
        col_blocks.append(across(white, "row", k))
    for k in range(2, column_count, 2):
        row_blocks[k] = across(white, "col", k)
    for k in range(0, column_count, 2):
        row_blocks[k + 1] = across(row_blocks[k], "col", 1)
    row_index = lax.axis_index("col") ^ jnp.arange(column_count, dtype=jnp.int32)
    col_index = lax.axis_index("row") ^ jnp.arange(row_count, dtype=jnp.int32)
    return pair_tiles(row_blocks, row_index, col_blocks, col_index, segments)


def solution(mesh):
    in_specs = (P(("row", "col"), None, None), P(("row", "col")), P(("row", "col")))
    out_specs = P(None, None, "row", "col")
    return jax.shard_map(shards, mesh=mesh, in_specs=in_specs, out_specs=out_specs, check_vma=False)
```

```python
import functools
import math

import jax
import jax.numpy as jnp
from jax import lax
from jax.experimental import pallas as pl
from jax.experimental.pallas import tpu as pltpu
from jax.sharding import PartitionSpec as P

power_floor = 0.25
bins = 3
lanes = 128
group = 8
slab = 8
full = 32767.0
vmem_bytes = 48 * 1024 * 1024

tail_tile = 2 * bins
width = (tail_tile + 1) * lanes


def meta_lane(segments):
    return tail_tile * (segments - lanes)


def dot_t(a, b):
    return lax.dot_general(a, b, (((1,), (1,)), ((), ())), preferred_element_type=jnp.float32)


def split(q):
    high = q.astype(jnp.bfloat16)
    return high, (q - high.astype(jnp.float32)).astype(jnp.bfloat16)


def iota(shape, dim):
    return lax.broadcasted_iota(jnp.int32, shape, dim)


def roll(x, shift):
    return pltpu.roll(x, shift % x.shape[1], 1)


def whiten_kernel(home_rows, parts, count_ref, ids_ref, source_ref, out_ref, x_ref, weight_ref, id_ref, coded_ref, found_ref, sems):
    slot_count, segments, two_band = x_ref.shape
    edges = [slot_count * e // parts[-1] for e in parts]
    copies = []
    for c in range(len(parts) - 1):
        span = pl.ds(edges[c], edges[c + 1] - edges[c])
        copies.append(pltpu.make_async_copy(source_ref.at[span], x_ref.at[span], sems.at[c]))
        copies[c].start()
    band = two_band // 2
    tail = segments - lanes
    depth = group * two_band

    row = iota((lanes, depth), 0)
    col = iota((lanes, depth), 1)
    part = row // group
    same = (row % group) == (col // two_band)
    lane = col % two_band
    lower = (part // 2) * (band // 4)
    center = (part % 2) * band + lower + band // 4
    picks = same & (part < 2 * bins) & (lane == center)
    weight_ref[:, :depth] = jnp.where(picks, 1.0, 0.0).astype(jnp.bfloat16)
    half = depth // 2
    row = iota((lanes, half), 0)
    col = iota((lanes, half), 1)
    part = row // group
    lower = (part - 2 * bins) * (band // 4)
    within = col % band
    inside = (row % group == col // band) & (part >= 2 * bins) & (part < 3 * bins)
    inside = inside & (within >= lower) & (within < lower + band // 2)
    window = jnp.where(inside, 1.0, 0.0).astype(jnp.bfloat16)
    weight_ref[:, depth : depth + half] = window
    weight_ref[:, depth + half :] = window
    left = iota((segments, two_band), 1) < band
    ids = ids_ref[...].astype(jnp.float32)
    local = ids - home_rows * jnp.floor((ids + 0.5) * (1.0 / home_rows))
    eye = iota((slot_count, slot_count), 0) == iota((slot_count, slot_count), 1)
    id_ref[...] = jnp.sum(jnp.where(eye, local + 1.0, 0.0), axis=1, keepdims=True)

    target = jnp.floor((ids + 0.5) * (1.0 / home_rows))
    shape = (slot_count, slot_count)
    j = iota(shape, 0)
    i = iota(shape, 1)
    target_column = jnp.sum(jnp.where(j == i, target, 0.0), axis=1, keepdims=True)
    count = count_ref[0]
    ahead = (j < i) & (j < count) & (target_column == target)
    within = jnp.sum(jnp.where(ahead, 1.0, 0.0), axis=0, keepdims=True)
    live = iota((1, slot_count), 1) < count
    place = jnp.where(live, target * slab + within, -1.0)
    send_rows = out_ref.shape[0]
    spot = iota((send_rows, slot_count), 0).astype(jnp.float32)
    chosen = jnp.where(spot == place, 1.0, 0.0).astype(jnp.bfloat16)

    for c in range(len(parts) - 1):
        copies[c].wait()
        for start in range(edges[c], edges[c + 1], group):
            x = x_ref[start : start + group]
            xs = jnp.concatenate([x[s] for s in range(group)], axis=1)
            folded = []
            for s in range(0, group, 2):
                pair = []
                for xf in (x[s].astype(jnp.float32), x[s + 1].astype(jnp.float32)):
                    energy = xf * xf
                    pair.append(energy + roll(energy, band))
                folded.append(jnp.where(left, pair[0], pair[1]))
            folded = jnp.concatenate(folded, axis=1)
            high = folded.astype(jnp.bfloat16)
            low = (folded - high.astype(jnp.float32)).astype(jnp.bfloat16)
            got = dot_t(jnp.concatenate([xs, high, low], axis=1), weight_ref[...]).T
            for t in range(3 * bins):
                found_ref[t, start : start + group] = got[t * group : (t + 1) * group]

    halves = 2
    for half in range(halves):
        span = slice(half * slot_count // halves, (half + 1) * slot_count // halves)
        last = []
        mants = []
        expos = []
        for f in range(bins):
            gain = lax.rsqrt(jnp.maximum(found_ref[2 * bins + f, span] * (2.0 / band), power_floor))
            pair = [found_ref[2 * f, span] * gain, found_ref[2 * f + 1, span] * gain]
            size = jnp.maximum(jnp.abs(pair[0]), jnp.abs(pair[1]))
            peak = jnp.maximum(jnp.max(size, axis=1, keepdims=True), 1e-30)
            expo = jnp.ceil(jnp.log2(peak))
            mant = jnp.floor(peak * jnp.exp2(-expo) * 16384.0) + 1.0
            inverse = (full * 16384.0) / (mant * jnp.exp2(expo))
            expos.append(expo)
            mants.append(mant)
            for p in range(2):
                q = jnp.clip(jnp.round(pair[p] * inverse), -full, full)
                t = 2 * f + p
                coded_ref[span, t * lanes : (t + 1) * lanes] = q[:, :lanes]
                last.append(q[:, lanes:])
        last += mants + expos + [id_ref[span, :]]
        used = tail_tile * tail + 2 * bins + 1
        last.append(jnp.zeros((slot_count // halves, lanes - used), jnp.float32))
        coded_ref[span, tail_tile * lanes :] = jnp.concatenate(last, axis=1)

    high, low = split(coded_ref[...])
    sent = jnp.dot(chosen, high, preferred_element_type=jnp.float32)
    sent += jnp.dot(chosen, low, preferred_element_type=jnp.float32)
    out_ref[...] = sent.astype(jnp.int32).astype(jnp.int16)


def whiten_pack(spectra, station_ids, counts, readers):
    slot_count, segments, two_band = spectra.shape
    home_rows = slot_count // 2
    parts = (0, 1, 3)
    return pl.pallas_call(
        functools.partial(whiten_kernel, home_rows, parts),
        out_shape=jax.ShapeDtypeStruct((readers * slab, width), jnp.int16),
        in_specs=[
            pl.BlockSpec(memory_space=pltpu.SMEM),
            pl.BlockSpec(memory_space=pltpu.VMEM),
            pl.BlockSpec(memory_space=pl.ANY),
        ],
        out_specs=pl.BlockSpec(memory_space=pltpu.VMEM),
        scratch_shapes=[
            pltpu.VMEM(spectra.shape, spectra.dtype),
            pltpu.VMEM((lanes, 2 * group * two_band), jnp.bfloat16),
            pltpu.VMEM((slot_count, 1), jnp.float32),
            pltpu.VMEM((slot_count, width), jnp.float32),
            pltpu.VMEM((3 * bins, slot_count, segments), jnp.float32),
            pltpu.SemaphoreType.DMA((len(parts) - 1,)),
        ],
        compiler_params=pltpu.CompilerParams(vmem_limit_bytes=vmem_bytes),
        name="whiten_pack",
    )(counts, station_ids.reshape(1, slot_count), spectra)


def settle_kernel(id_lane, in_ref, out_ref):
    home_rows = out_ref.shape[0]
    q = in_ref[...].astype(jnp.int32).astype(jnp.float32)
    station = q[:, id_lane : id_lane + 1]
    wanted = (iota((q.shape[0], home_rows), 1) + 1).astype(jnp.float32)
    chosen = jnp.where(station == wanted, 1.0, 0.0).astype(jnp.bfloat16)
    high, low = split(q)
    dims = (((0,), (0,)), ((), ()))
    home = lax.dot_general(chosen, high, dims, preferred_element_type=jnp.float32)
    home += lax.dot_general(chosen, low, dims, preferred_element_type=jnp.float32)
    out_ref[...] = home.astype(jnp.int32).astype(jnp.int16)


def settle(received, home_rows, segments):
    id_lane = tail_tile * lanes + meta_lane(segments) + 2 * bins
    return pl.pallas_call(
        functools.partial(settle_kernel, id_lane),
        out_shape=jax.ShapeDtypeStruct((home_rows, width), jnp.int16),
        compiler_params=pltpu.CompilerParams(vmem_limit_bytes=vmem_bytes),
        name="settle",
    )(received)


def pair_kernel(segments, row_n, col_n, place_ref, *refs):
    row_refs = refs[:row_n]
    col_refs = refs[row_n : row_n + col_n]
    out_ref, a_ref, b_ref, scale_ref, tail_ref = refs[row_n + col_n :]
    f = pl.program_id(0)
    home_rows = row_refs[0].shape[0]
    tail = segments - lanes
    meta = meta_lane(segments)
    columns = col_n * home_rows
    lane = iota((home_rows, lanes), 1)
    unit = 1.0 / (16384.0 * full)

    def load(ref):
        start = pl.multiple_of(f * 2 * lanes, 2 * lanes)
        main = ref[:, pl.ds(start, 2 * lanes)].astype(jnp.int32).astype(jnp.float32)
        last = ref[:, tail_tile * lanes :].astype(jnp.int32).astype(jnp.float32)
        mine = pltpu.roll(last, lax.rem(lanes - f * 2 * tail, lanes), 1)
        return main, last, jnp.where(lane < 2 * tail, mine, 0.0)

    def ends(first, second, third):
        return first + roll(second, 2 * tail) + roll(third, 4 * tail)

    def wide(x):
        return x[0].astype(jnp.float32), x[1].astype(jnp.float32)

    for k in range(row_n):
        main, last, mine = load(row_refs[k])
        start = pl.multiple_of(place_ref[0, k] * home_rows, home_rows)
        high, low = split(main)
        tail_high, tail_low = wide(split(mine))
        ending = ends(tail_high, tail_low, tail_high).astype(jnp.bfloat16)
        a_ref[pl.ds(start, home_rows), :] = jnp.concatenate([high, low, high, ending], axis=1)
        power = last * jnp.exp2(roll(last, -bins))
        scale = jnp.sum(jnp.where(lane == meta + f, power, 0.0), axis=1, keepdims=True)
        scale_ref[pl.ds(start, home_rows), :] = scale * unit

    for k in range(col_n):
        main, last, mine = load(col_refs[k])
        turned = jnp.concatenate([-main[:, lanes:], main[:, :lanes]], axis=1)
        mine_turned = jnp.where(lane < tail, -roll(mine, -tail), roll(mine, tail))
        mine_turned = jnp.where(lane < 2 * tail, mine_turned, 0.0)
        start = pl.multiple_of(place_ref[1, k] * home_rows, home_rows)
        for offset, value, end in ((0, main, mine), (columns, turned, mine_turned)):
            high, low = split(value)
            tail_high, tail_low = wide(split(end))
            ending = ends(tail_high, tail_high, tail_low).astype(jnp.bfloat16)
            b_ref[pl.ds(offset + start, home_rows), :] = jnp.concatenate([high, high, low, ending], axis=1)
        tail_ref[pl.ds(start, home_rows), :] = last

    pick = iota((8, lanes), 0)
    want = jnp.where(pick == 0, meta + f, meta + bins + f)
    chosen = jnp.where((iota((8, lanes), 1) == want) & (pick < 2), 1.0, 0.0).astype(jnp.bfloat16)
    high, low = split(tail_ref[...])
    codes = dot_t(chosen, high) + dot_t(chosen, low)
    column_scale = codes[0:1] * jnp.exp2(codes[1:2]) * (unit / math.sqrt(segments))

    product = dot_t(a_ref[...], b_ref[...])
    row_scale = scale_ref[...]
    for p in range(2):
        value = product[:, p * columns : (p + 1) * columns] * row_scale * column_scale
        out_ref[0, p] = value.astype(jnp.bfloat16)


def pair_tiles(row_blocks, row_index, col_blocks, col_index, segments):
    row_n, col_n = len(row_blocks), len(col_blocks)
    home_rows = row_blocks[0].shape[0]
    rows, columns = row_n * home_rows, col_n * home_rows
    most = max(row_n, col_n)
    place = jnp.stack([
        jnp.pad(row_index, (0, most - row_n)),
        jnp.pad(col_index, (0, most - col_n)),
    ])
    block = pl.BlockSpec((home_rows, width), lambda f, place: (0, 0))
    depth = 7 * lanes
    return pl.pallas_call(
        functools.partial(pair_kernel, segments, row_n, col_n),
        grid_spec=pltpu.PrefetchScalarGridSpec(
            num_scalar_prefetch=1,
            grid=(bins,),
            in_specs=[block] * (row_n + col_n),
            out_specs=pl.BlockSpec((1, 2, rows, columns), lambda f, place: (f, 0, 0, 0)),
            scratch_shapes=[
                pltpu.VMEM((rows, depth), jnp.bfloat16),
                pltpu.VMEM((2 * columns, depth), jnp.bfloat16),
                pltpu.VMEM((rows, 1), jnp.float32),
                pltpu.VMEM((columns, lanes), jnp.float32),
            ],
        ),
        out_shape=jax.ShapeDtypeStruct((bins, 2, rows, columns), jnp.bfloat16),
        compiler_params=pltpu.CompilerParams(vmem_limit_bytes=vmem_bytes),
        name="pair_tiles",
    )(place, *row_blocks, *col_blocks)


def across(value, axis, distance):
    size = lax.axis_size(axis)
    return lax.ppermute(value, axis, [(i, i ^ distance) for i in range(size)])


def gather_rows(white, count):
    blocks = {0: white}
    distance = 2
    while distance < count:
        for k in range(0, distance, 2):
            blocks[k + distance] = across(blocks[k], "col", distance)
        distance *= 2
    for k in range(0, count, 2):
        blocks[k + 1] = across(blocks[k], "col", 1)
    return [blocks[k] for k in range(count)]


def shards(spectra, station_ids, counts):
    row_count = lax.axis_size("row")
    column_count = lax.axis_size("col")
    readers = row_count * column_count
    slot_count, segments, _ = spectra.shape
    home_rows = slot_count // 2
    packed = whiten_pack(spectra, station_ids, counts, readers)
    received = lax.all_to_all(packed, ("row", "col"), split_axis=0, concat_axis=0, tiled=True)
    white = settle(received, home_rows, segments)
    row_blocks = gather_rows(white, column_count)
    col_blocks = [white] + [across(white, "row", k) for k in range(1, row_count)]
    row_index = lax.axis_index("col") ^ jnp.arange(column_count, dtype=jnp.int32)
    col_index = lax.axis_index("row") ^ jnp.arange(row_count, dtype=jnp.int32)
    return pair_tiles(row_blocks, row_index, col_blocks, col_index, segments)


def solution(mesh):
    in_specs = (P(("row", "col"), None, None), P(("row", "col")), P(("row", "col")))
    out_specs = P(None, None, "row", "col")
    return jax.shard_map(shards, mesh=mesh, in_specs=in_specs, out_specs=out_specs, check_vma=False)
```

```python
import functools
import math

import jax
import jax.numpy as jnp
from jax import lax
from jax.experimental import pallas as pl
from jax.experimental.pallas import tpu as pltpu
from jax.sharding import PartitionSpec as P

power_floor = 0.25
bins = 3
lanes = 128
group = 8
slab = 8
full = 32767.0
vmem_bytes = 48 * 1024 * 1024

tail_tile = 2 * bins
main_width = tail_tile * lanes
width = (tail_tile + 1) * lanes


def meta_lane(segments):
    return tail_tile * (segments - lanes)


def dot_t(a, b):
    return lax.dot_general(a, b, (((1,), (1,)), ((), ())), preferred_element_type=jnp.float32)


def split(q):
    high = q.astype(jnp.bfloat16)
    return high, (q - high.astype(jnp.float32)).astype(jnp.bfloat16)


def iota(shape, dim):
    return lax.broadcasted_iota(jnp.int32, shape, dim)


def roll(x, shift):
    return pltpu.roll(x, shift % x.shape[1], 1)


def whiten_kernel(home_rows, parts, count_ref, ids_ref, source_ref, out_ref, x_ref, weight_ref, id_ref, coded_ref, found_ref, stage_ref, ends_ref, sems):
    slot_count, segments, two_band = x_ref.shape
    edges = [slot_count * e // parts[-1] for e in parts]
    copies = []
    for c in range(len(parts) - 1):
        span = pl.ds(edges[c], edges[c + 1] - edges[c])
        copies.append(pltpu.make_async_copy(source_ref.at[span], x_ref.at[span], sems.at[c]))
        copies[c].start()
    band = two_band // 2
    tail = segments - lanes
    depth = group * two_band

    row = iota((lanes, depth), 0)
    col = iota((lanes, depth), 1)
    part = row // group
    same = (row % group) == (col // two_band)
    lane = col % two_band
    lower = (part // 2) * (band // 4)
    center = (part % 2) * band + lower + band // 4
    picks = same & (part < 2 * bins) & (lane == center)
    weight_ref[:, :depth] = jnp.where(picks, 1.0, 0.0).astype(jnp.bfloat16)
    half = depth // 2
    row = iota((lanes, half), 0)
    col = iota((lanes, half), 1)
    part = row // group
    lower = (part - 2 * bins) * (band // 4)
    within = col % band
    inside = (row % group == col // band) & (part >= 2 * bins) & (part < 3 * bins)
    inside = inside & (within >= lower) & (within < lower + band // 2)
    window = jnp.where(inside, 1.0, 0.0).astype(jnp.bfloat16)
    weight_ref[:, depth : depth + half] = window
    weight_ref[:, depth + half :] = window
    left = iota((segments, two_band), 1) < band
    ids = ids_ref[...].astype(jnp.float32)
    local = ids - home_rows * jnp.floor((ids + 0.5) * (1.0 / home_rows))
    eye = iota((slot_count, slot_count), 0) == iota((slot_count, slot_count), 1)
    id_ref[...] = jnp.sum(jnp.where(eye, local + 1.0, 0.0), axis=1, keepdims=True)

    target = jnp.floor((ids + 0.5) * (1.0 / home_rows))
    shape = (slot_count, slot_count)
    j = iota(shape, 0)
    i = iota(shape, 1)
    target_column = jnp.sum(jnp.where(j == i, target, 0.0), axis=1, keepdims=True)
    count = count_ref[0]
    ahead = (j < i) & (j < count) & (target_column == target)
    within = jnp.sum(jnp.where(ahead, 1.0, 0.0), axis=0, keepdims=True)
    live = iota((1, slot_count), 1) < count
    place = jnp.where(live, target * slab + within, -1.0)
    send_rows = out_ref.shape[0]
    spot = iota((send_rows, slot_count), 0).astype(jnp.float32)
    chosen = jnp.where(spot == place, 1.0, 0.0).astype(jnp.bfloat16)

    for c in range(len(parts) - 1):
        copies[c].wait()
        for start in range(edges[c], edges[c + 1], group):
            x = x_ref[start : start + group]
            xs = jnp.concatenate([x[s] for s in range(group)], axis=1)
            folded = []
            for s in range(0, group, 2):
                pair = []
                for xf in (x[s].astype(jnp.float32), x[s + 1].astype(jnp.float32)):
                    energy = xf * xf
                    pair.append(energy + roll(energy, band))
                folded.append(jnp.where(left, pair[0], pair[1]))
            folded = jnp.concatenate(folded, axis=1)
            high = folded.astype(jnp.bfloat16)
            low = (folded - high.astype(jnp.float32)).astype(jnp.bfloat16)
            got = dot_t(jnp.concatenate([xs, high, low], axis=1), weight_ref[...]).T
            for t in range(3 * bins):
                found_ref[t, start : start + group] = got[t * group : (t + 1) * group]

    halves = 2
    for half in range(halves):
        span = slice(half * slot_count // halves, (half + 1) * slot_count // halves)
        last = []
        mants = []
        expos = []
        for f in range(bins):
            gain = lax.rsqrt(jnp.maximum(found_ref[2 * bins + f, span] * (2.0 / band), power_floor))
            pair = [found_ref[2 * f, span] * gain, found_ref[2 * f + 1, span] * gain]
            size = jnp.maximum(jnp.abs(pair[0]), jnp.abs(pair[1]))
            peak = jnp.maximum(jnp.max(size, axis=1, keepdims=True), 1e-30)
            expo = jnp.ceil(jnp.log2(peak))
            mant = jnp.floor(peak * jnp.exp2(-expo) * 16384.0) + 1.0
            inverse = (full * 16384.0) / (mant * jnp.exp2(expo))
            expos.append(expo)
            mants.append(mant)
            for p in range(2):
                q = jnp.clip(jnp.round(pair[p] * inverse), -full, full)
                t = 2 * f + p
                coded_ref[span, t * lanes : (t + 1) * lanes] = q[:, :lanes]
                last.append(q[:, lanes:])
        last += mants + expos + [id_ref[span, :]]
        used = tail_tile * tail + 2 * bins + 1
        last.append(jnp.zeros((slot_count // halves, lanes - used), jnp.float32))
        coded_ref[span, tail_tile * lanes :] = jnp.concatenate(last, axis=1)

    high, low = split(coded_ref[...])
    sent = jnp.dot(chosen, high, preferred_element_type=jnp.float32)
    sent += jnp.dot(chosen, low, preferred_element_type=jnp.float32)
    for t in range(tail_tile):
        stage_ref[t] = sent[:, t * lanes : (t + 1) * lanes]
    ends_ref[...] = sent[:, main_width:]
    readers = send_rows // slab
    for j in range(tail_tile):
        from_rows = ends_ref[pl.ds(j, readers, stride=slab), :]
        stage_ref[j, pl.ds(tail_tile, readers, stride=slab), :] = from_rows
    for t in range(tail_tile):
        out_ref[:, t * lanes : (t + 1) * lanes] = stage_ref[t].astype(jnp.int32).astype(jnp.int16)


def whiten_pack(spectra, station_ids, counts, readers):
    slot_count, segments, two_band = spectra.shape
    home_rows = slot_count // 2
    parts = (0, 1, 3)
    return pl.pallas_call(
        functools.partial(whiten_kernel, home_rows, parts),
        out_shape=jax.ShapeDtypeStruct((readers * slab, main_width), jnp.int16),
        in_specs=[
            pl.BlockSpec(memory_space=pltpu.SMEM),
            pl.BlockSpec(memory_space=pltpu.VMEM),
            pl.BlockSpec(memory_space=pl.ANY),
        ],
        out_specs=pl.BlockSpec(memory_space=pltpu.VMEM),
        scratch_shapes=[
            pltpu.VMEM(spectra.shape, spectra.dtype),
            pltpu.VMEM((lanes, 2 * group * two_band), jnp.bfloat16),
            pltpu.VMEM((slot_count, 1), jnp.float32),
            pltpu.VMEM((slot_count, width), jnp.float32),
            pltpu.VMEM((3 * bins, slot_count, segments), jnp.float32),
            pltpu.VMEM((tail_tile, readers * slab, lanes), jnp.float32),
            pltpu.VMEM((readers * slab, lanes), jnp.float32),
            pltpu.SemaphoreType.DMA((len(parts) - 1,)),
        ],
        compiler_params=pltpu.CompilerParams(vmem_limit_bytes=vmem_bytes),
        name="whiten_pack",
    )(counts, station_ids.reshape(1, slot_count), spectra)


def settle_kernel(id_lane, in_ref, out_ref, stage_ref, ends_ref):
    home_rows = out_ref.shape[0]
    rows = in_ref.shape[0]
    readers = rows // slab
    for t in range(tail_tile):
        stage_ref[t] = in_ref[:, t * lanes : (t + 1) * lanes].astype(jnp.int32).astype(jnp.float32)
    ends_ref[...] = jnp.zeros_like(ends_ref)
    for j in range(tail_tile):
        from_rows = stage_ref[j, pl.ds(tail_tile, readers, stride=slab), :]
        ends_ref[pl.ds(j, readers, stride=slab), :] = from_rows
    ends = ends_ref[...]
    station = ends[:, id_lane : id_lane + 1]
    wanted = (iota((rows, home_rows), 1) + 1).astype(jnp.float32)
    chosen = jnp.where(station == wanted, 1.0, 0.0).astype(jnp.bfloat16)
    dims = (((0,), (0,)), ((), ()))
    high, low = split(jnp.concatenate([stage_ref[t] for t in range(tail_tile)] + [ends], axis=1))
    home = lax.dot_general(chosen, high, dims, preferred_element_type=jnp.float32)
    home += lax.dot_general(chosen, low, dims, preferred_element_type=jnp.float32)
    out_ref[...] = home.astype(jnp.int32).astype(jnp.int16)


def settle(received, home_rows, segments):
    return pl.pallas_call(
        functools.partial(settle_kernel, meta_lane(segments) + 2 * bins),
        out_shape=jax.ShapeDtypeStruct((home_rows, width), jnp.int16),
        scratch_shapes=[
            pltpu.VMEM((tail_tile, received.shape[0], lanes), jnp.float32),
            pltpu.VMEM((received.shape[0], lanes), jnp.float32),
        ],
        compiler_params=pltpu.CompilerParams(vmem_limit_bytes=vmem_bytes),
        name="settle",
    )(received)


def ends_of(last, f, tail):
    mine = last if f == 0 else roll(last, -f * 2 * tail)
    return jnp.where(iota(mine.shape, 1) < 2 * tail, mine, 0.0)


def line_up(first, second, third, tail):
    ending = first.astype(jnp.float32) + roll(second.astype(jnp.float32), 2 * tail)
    return (ending + roll(third.astype(jnp.float32), 4 * tail)).astype(jnp.bfloat16)


def wide(ref, start, size):
    return ref[:, start : start + size].astype(jnp.int32).astype(jnp.float32)


def rows_kernel(segments, row_n, place_ref, *refs):
    row_refs = refs[:row_n]
    a_ref, scale_ref = refs[row_n:]
    home_rows = row_refs[0].shape[0]
    tail = segments - lanes
    for k in range(row_n):
        start = pl.multiple_of(place_ref[0, k] * home_rows, home_rows)
        span = pl.ds(start, home_rows)
        last = wide(row_refs[k], main_width, lanes)
        scale_ref[span, :] = last * jnp.exp2(roll(last, -bins)) * (1.0 / (16384.0 * full))
        for f in range(bins):
            high, low = split(wide(row_refs[k], 2 * f * lanes, 2 * lanes))
            tail_high, tail_low = split(ends_of(last, f, tail))
            ending = line_up(tail_high, tail_low, tail_high, tail)
            a_ref[f, span, :] = jnp.concatenate([high, low, high, ending], axis=1)


def pair_kernel(segments, col_n, place_ref, a_ref, scale_ref, *refs):
    col_refs = refs[:col_n]
    out_ref, b_ref, codes_ref, tile_ref, sems = refs[col_n:]
    home_rows = col_refs[0].shape[0]
    tail = segments - lanes
    meta = meta_lane(segments)
    columns = col_n * home_rows
    unit = 1.0 / (16384.0 * full * math.sqrt(segments))
    spans = []
    for k in range(col_n):
        spans.append(pl.multiple_of(place_ref[1, k] * home_rows, home_rows))
        codes_ref[pl.ds(spans[k], home_rows), :] = wide(col_refs[k], main_width, lanes)
    pick = iota((8, lanes), 0)
    chosen = jnp.where((iota((8, lanes), 1) == meta + pick) & (pick < 2 * bins), 1.0, 0.0).astype(jnp.bfloat16)
    high, low = split(codes_ref[...])
    codes = dot_t(chosen, high) + dot_t(chosen, low)

    copies = []
    for f in range(bins):
        slot = f % 2
        for k in range(col_n):
            last = wide(col_refs[k], main_width, lanes)
            high, low = split(wide(col_refs[k], 2 * f * lanes, 2 * lanes))
            mine = ends_of(last, f, tail)
            lane = iota(mine.shape, 1)
            turned = jnp.where(lane < tail, -roll(mine, -tail), roll(mine, tail))
            turned = jnp.where(lane < 2 * tail, turned, 0.0)
            tail_high, tail_low = split(mine)
            ending = line_up(tail_high, tail_high, tail_low, tail)
            b_ref[slot, pl.ds(spans[k], home_rows), :] = jnp.concatenate([high, high, low, ending], axis=1)
            high = jnp.concatenate([-high[:, lanes:], high[:, :lanes]], axis=1)
            low = jnp.concatenate([-low[:, lanes:], low[:, :lanes]], axis=1)
            tail_high, tail_low = split(turned)
            ending = line_up(tail_high, tail_high, tail_low, tail)
            b_ref[slot, pl.ds(columns + spans[k], home_rows), :] = jnp.concatenate([high, high, low, ending], axis=1)
        column_scale = codes[f : f + 1] * jnp.exp2(codes[bins + f : bins + f + 1]) * unit
        row_scale = scale_ref[:, meta + f : meta + f + 1]
        product = dot_t(a_ref[f], b_ref[slot])
        for p in range(2):
            value = product[:, p * columns : (p + 1) * columns] * row_scale * column_scale
            tile_ref[f, p] = value.astype(jnp.bfloat16)
        copies.append(pltpu.make_async_copy(tile_ref.at[f], out_ref.at[f], sems.at[f]))
        copies[f].start()
    for copy in copies:
        copy.wait()


def prepare_rows(place, row_blocks, segments):
    row_n = len(row_blocks)
    rows = row_n * row_blocks[0].shape[0]
    vmem = pl.BlockSpec(memory_space=pltpu.VMEM)
    return pl.pallas_call(
        functools.partial(rows_kernel, segments, row_n),
        out_shape=(
            jax.ShapeDtypeStruct((bins, rows, width), jnp.bfloat16),
            jax.ShapeDtypeStruct((rows, lanes), jnp.float32),
        ),
        in_specs=[pl.BlockSpec(memory_space=pltpu.SMEM)] + [vmem] * row_n,
        out_specs=(vmem, vmem),
        compiler_params=pltpu.CompilerParams(vmem_limit_bytes=vmem_bytes),
        cost_estimate=pl.CostEstimate(flops=1, bytes_accessed=1, transcendentals=0),
        name="prepare_rows",
    )(place, *row_blocks)


def pair_tiles(place, row_parts, row_scales, col_blocks, segments):
    col_n = len(col_blocks)
    rows = row_scales.shape[0]
    columns = col_n * col_blocks[0].shape[0]
    vmem = pl.BlockSpec(memory_space=pltpu.VMEM)
    return pl.pallas_call(
        functools.partial(pair_kernel, segments, col_n),
        in_specs=[pl.BlockSpec(memory_space=pltpu.SMEM)] + [vmem] * (2 + col_n),
        out_specs=pl.BlockSpec(memory_space=pl.ANY),
        scratch_shapes=[
            pltpu.VMEM((2, 2 * columns, width), jnp.bfloat16),
            pltpu.VMEM((columns, lanes), jnp.float32),
            pltpu.VMEM((bins, 2, rows, columns), jnp.bfloat16),
            pltpu.SemaphoreType.DMA((bins,)),
        ],
        out_shape=jax.ShapeDtypeStruct((bins, 2, rows, columns), jnp.bfloat16),
        compiler_params=pltpu.CompilerParams(vmem_limit_bytes=vmem_bytes),
        name="pair_tiles",
    )(place, row_parts, row_scales, *col_blocks)


def across(value, axis, distance):
    size = lax.axis_size(axis)
    return lax.ppermute(value, axis, [(i, i ^ distance) for i in range(size)])


def gather_columns(white, count):
    blocks = {0: white}
    distance = count // 2
    while distance:
        for k in list(blocks):
            blocks[k + distance] = across(blocks[k], "row", distance)
        distance //= 2
    return [blocks[k] for k in range(count)]


def gather_rows(white, count):
    blocks = {0: white}
    distance = 2
    while distance < count:
        for k in range(0, distance, 2):
            blocks[k + distance] = across(blocks[k], "col", distance)
        distance *= 2
    for k in range(0, count, 2):
        blocks[k + 1] = across(blocks[k], "col", 1)
    return [blocks[k] for k in range(count)]


def shards(spectra, station_ids, counts):
    row_count = lax.axis_size("row")
    column_count = lax.axis_size("col")
    readers = row_count * column_count
    slot_count, segments, _ = spectra.shape
    home_rows = slot_count // 2
    packed = whiten_pack(spectra, station_ids, counts, readers)
    received = lax.all_to_all(packed, ("row", "col"), split_axis=0, concat_axis=0, tiled=True)
    white = settle(received, home_rows, segments)
    row_blocks = gather_rows(white, column_count)
    col_blocks = gather_columns(white, row_count)
    most = jnp.arange(max(row_count, column_count), dtype=jnp.int32)
    place = jnp.stack([lax.axis_index("col") ^ most, lax.axis_index("row") ^ most])
    row_parts, row_scales = prepare_rows(place, row_blocks, segments)
    return pair_tiles(place, row_parts, row_scales, col_blocks, segments)


def solution(mesh):
    in_specs = (P(("row", "col"), None, None), P(("row", "col")), P(("row", "col")))
    out_specs = P(None, None, "row", "col")
    return jax.shard_map(shards, mesh=mesh, in_specs=in_specs, out_specs=out_specs, check_vma=False)
```

```python
import functools
import math

import jax
import jax.numpy as jnp
from jax import lax
from jax.experimental import pallas as pl
from jax.experimental.pallas import tpu as pltpu
from jax.sharding import PartitionSpec as P

power_floor = 0.25
bins = 3
lanes = 128
group = 8
slab = 8
full = 32767.0
vmem_bytes = 48 * 1024 * 1024

tail_tile = 2 * bins
main_width = tail_tile * lanes
width = (tail_tile + 1) * lanes


def meta_lane(segments):
    return tail_tile * (segments - lanes)


def dot_t(a, b):
    return lax.dot_general(a, b, (((1,), (1,)), ((), ())), preferred_element_type=jnp.float32)


def split(q):
    high = q.astype(jnp.bfloat16)
    return high, (q - high.astype(jnp.float32)).astype(jnp.bfloat16)


def iota(shape, dim):
    return lax.broadcasted_iota(jnp.int32, shape, dim)


def roll(x, shift):
    return pltpu.roll(x, shift % x.shape[1], 1)


def whiten_kernel(home_rows, parts, count_ref, ids_ref, source_ref, out_ref, x_ref, weight_ref, id_ref, coded_ref, found_ref, stage_ref, ends_ref, sems):
    slot_count, segments, two_band = x_ref.shape
    edges = [slot_count * e // parts[-1] for e in parts]
    copies = []
    for c in range(len(parts) - 1):
        span = pl.ds(edges[c], edges[c + 1] - edges[c])
        copies.append(pltpu.make_async_copy(source_ref.at[span], x_ref.at[span], sems.at[c]))
        copies[c].start()
    band = two_band // 2
    tail = segments - lanes
    depth = group * two_band

    row = iota((lanes, depth), 0)
    col = iota((lanes, depth), 1)
    part = row // group
    same = (row % group) == (col // two_band)
    lane = col % two_band
    lower = (part // 2) * (band // 4)
    center = (part % 2) * band + lower + band // 4
    picks = same & (part < 2 * bins) & (lane == center)
    weight_ref[:, :depth] = jnp.where(picks, 1.0, 0.0).astype(jnp.bfloat16)
    half = depth // 2
    row = iota((lanes, half), 0)
    col = iota((lanes, half), 1)
    part = row // group
    lower = (part - 2 * bins) * (band // 4)
    within = col % band
    inside = (row % group == col // band) & (part >= 2 * bins) & (part < 3 * bins)
    inside = inside & (within >= lower) & (within < lower + band // 2)
    window = jnp.where(inside, 1.0, 0.0).astype(jnp.bfloat16)
    weight_ref[:, depth : depth + half] = window
    weight_ref[:, depth + half :] = window
    left = iota((segments, two_band), 1) < band
    ids = ids_ref[...].astype(jnp.float32)
    local = ids - home_rows * jnp.floor((ids + 0.5) * (1.0 / home_rows))
    eye = iota((slot_count, slot_count), 0) == iota((slot_count, slot_count), 1)
    id_ref[...] = jnp.sum(jnp.where(eye, local + 1.0, 0.0), axis=1, keepdims=True)

    target = jnp.floor((ids + 0.5) * (1.0 / home_rows))
    shape = (slot_count, slot_count)
    j = iota(shape, 0)
    i = iota(shape, 1)
    target_column = jnp.sum(jnp.where(j == i, target, 0.0), axis=1, keepdims=True)
    count = count_ref[0]
    ahead = (j < i) & (j < count) & (target_column == target)
    within = jnp.sum(jnp.where(ahead, 1.0, 0.0), axis=0, keepdims=True)
    live = iota((1, slot_count), 1) < count
    place = jnp.where(live, target * slab + within, -1.0)
    send_rows = out_ref.shape[0]
    spot = iota((send_rows, slot_count), 0).astype(jnp.float32)
    chosen = jnp.where(spot == place, 1.0, 0.0).astype(jnp.bfloat16)

    for c in range(len(parts) - 1):
        copies[c].wait()
        for start in range(edges[c], edges[c + 1], group):
            x = x_ref[start : start + group]
            xs = jnp.concatenate([x[s] for s in range(group)], axis=1)
            folded = []
            for s in range(0, group, 2):
                first = x[s]
                second = x[s + 1]
                near = jnp.concatenate([first[:, :band], second[:, band:]], axis=1).astype(jnp.float32)
                far = jnp.concatenate([first[:, band:], second[:, :band]], axis=1).astype(jnp.float32)
                folded.append(near * near + far * far)
            folded = jnp.concatenate(folded, axis=1)
            high = folded.astype(jnp.bfloat16)
            low = (folded - high.astype(jnp.float32)).astype(jnp.bfloat16)
            got = dot_t(jnp.concatenate([xs, high, low], axis=1), weight_ref[...]).T
            for t in range(3 * bins):
                found_ref[t, start : start + group] = got[t * group : (t + 1) * group]

    halves = 2
    for half in range(halves):
        span = slice(half * slot_count // halves, (half + 1) * slot_count // halves)
        last = []
        mants = []
        expos = []
        for f in range(bins):
            gain = lax.rsqrt(jnp.maximum(found_ref[2 * bins + f, span] * (2.0 / band), power_floor))
            pair = [found_ref[2 * f, span] * gain, found_ref[2 * f + 1, span] * gain]
            size = jnp.maximum(jnp.abs(pair[0]), jnp.abs(pair[1]))
            peak = jnp.maximum(jnp.max(size, axis=1, keepdims=True), 1e-30)
            expo = jnp.ceil(jnp.log2(peak))
            mant = jnp.floor(peak * jnp.exp2(-expo) * 16384.0) + 1.0
            inverse = (full * 16384.0) / (mant * jnp.exp2(expo))
            expos.append(expo)
            mants.append(mant)
            for p in range(2):
                q = jnp.clip(jnp.round(pair[p] * inverse), -full, full)
                t = 2 * f + p
                coded_ref[span, t * lanes : (t + 1) * lanes] = q[:, :lanes]
                last.append(q[:, lanes:])
        last += mants + expos + [id_ref[span, :]]
        used = tail_tile * tail + 2 * bins + 1
        last.append(jnp.zeros((slot_count // halves, lanes - used), jnp.float32))
        coded_ref[span, tail_tile * lanes :] = jnp.concatenate(last, axis=1)

    high, low = split(coded_ref[...])
    sent = jnp.dot(chosen, high, preferred_element_type=jnp.float32)
    sent += jnp.dot(chosen, low, preferred_element_type=jnp.float32)
    for t in range(tail_tile):
        stage_ref[t] = sent[:, t * lanes : (t + 1) * lanes]
    ends_ref[...] = sent[:, main_width:]
    readers = send_rows // slab
    for j in range(tail_tile):
        from_rows = ends_ref[pl.ds(j, readers, stride=slab), :]
        stage_ref[j, pl.ds(tail_tile, readers, stride=slab), :] = from_rows
    for t in range(tail_tile):
        out_ref[:, t * lanes : (t + 1) * lanes] = stage_ref[t].astype(jnp.int32).astype(jnp.int16)


def whiten_pack(spectra, station_ids, counts, readers):
    slot_count, segments, two_band = spectra.shape
    home_rows = slot_count // 2
    parts = (0, 1, 3)
    return pl.pallas_call(
        functools.partial(whiten_kernel, home_rows, parts),
        out_shape=jax.ShapeDtypeStruct((readers * slab, main_width), jnp.int16),
        in_specs=[
            pl.BlockSpec(memory_space=pltpu.SMEM),
            pl.BlockSpec(memory_space=pltpu.VMEM),
            pl.BlockSpec(memory_space=pl.ANY),
        ],
        out_specs=pl.BlockSpec(memory_space=pltpu.VMEM),
        scratch_shapes=[
            pltpu.VMEM(spectra.shape, spectra.dtype),
            pltpu.VMEM((lanes, 2 * group * two_band), jnp.bfloat16),
            pltpu.VMEM((slot_count, 1), jnp.float32),
            pltpu.VMEM((slot_count, width), jnp.float32),
            pltpu.VMEM((3 * bins, slot_count, segments), jnp.float32),
            pltpu.VMEM((tail_tile, readers * slab, lanes), jnp.float32),
            pltpu.VMEM((readers * slab, lanes), jnp.float32),
            pltpu.SemaphoreType.DMA((len(parts) - 1,)),
        ],
        compiler_params=pltpu.CompilerParams(vmem_limit_bytes=vmem_bytes),
        name="whiten_pack",
    )(counts, station_ids.reshape(1, slot_count), spectra)


def settle_kernel(id_lane, in_ref, out_ref, stage_ref, ends_ref):
    home_rows = out_ref.shape[0]
    rows = in_ref.shape[0]
    readers = rows // slab
    for t in range(tail_tile):
        stage_ref[t] = in_ref[:, t * lanes : (t + 1) * lanes].astype(jnp.int32).astype(jnp.float32)
    ends_ref[...] = jnp.zeros_like(ends_ref)
    for j in range(tail_tile):
        from_rows = stage_ref[j, pl.ds(tail_tile, readers, stride=slab), :]
        ends_ref[pl.ds(j, readers, stride=slab), :] = from_rows
    ends = ends_ref[...]
    station = ends[:, id_lane : id_lane + 1]
    wanted = (iota((rows, home_rows), 1) + 1).astype(jnp.float32)
    chosen = jnp.where(station == wanted, 1.0, 0.0).astype(jnp.bfloat16)
    dims = (((0,), (0,)), ((), ()))
    high, low = split(jnp.concatenate([stage_ref[t] for t in range(tail_tile)] + [ends], axis=1))
    home = lax.dot_general(chosen, high, dims, preferred_element_type=jnp.float32)
    home += lax.dot_general(chosen, low, dims, preferred_element_type=jnp.float32)
    out_ref[...] = home.astype(jnp.int32).astype(jnp.int16)


def settle(received, home_rows, segments):
    return pl.pallas_call(
        functools.partial(settle_kernel, meta_lane(segments) + 2 * bins),
        out_shape=jax.ShapeDtypeStruct((home_rows, width), jnp.int16),
        scratch_shapes=[
            pltpu.VMEM((tail_tile, received.shape[0], lanes), jnp.float32),
            pltpu.VMEM((received.shape[0], lanes), jnp.float32),
        ],
        compiler_params=pltpu.CompilerParams(vmem_limit_bytes=vmem_bytes),
        name="settle",
    )(received)


def ends_of(last, f, tail):
    mine = last if f == 0 else roll(last, -f * 2 * tail)
    return jnp.where(iota(mine.shape, 1) < 2 * tail, mine, 0.0)


def line_up(first, second, third, tail):
    ending = first.astype(jnp.float32) + roll(second.astype(jnp.float32), 2 * tail)
    return (ending + roll(third.astype(jnp.float32), 4 * tail)).astype(jnp.bfloat16)


def wide(ref, start, size):
    return ref[:, start : start + size].astype(jnp.int32).astype(jnp.float32)


def rows_kernel(segments, row_n, place_ref, *refs):
    row_refs = refs[:row_n]
    a_ref, scale_ref = refs[row_n:]
    home_rows = row_refs[0].shape[0]
    tail = segments - lanes
    for k in range(row_n):
        start = pl.multiple_of(place_ref[0, k] * home_rows, home_rows)
        span = pl.ds(start, home_rows)
        last = wide(row_refs[k], main_width, lanes)
        scale_ref[span, :] = last * jnp.exp2(roll(last, -bins)) * (1.0 / (16384.0 * full))
        for f in range(bins):
            high, low = split(wide(row_refs[k], 2 * f * lanes, 2 * lanes))
            tail_high, tail_low = split(ends_of(last, f, tail))
            ending = line_up(tail_high, tail_low, tail_high, tail)
            a_ref[f, span, :] = jnp.concatenate([high, low, high, ending], axis=1)


def pair_kernel(segments, col_n, place_ref, a_ref, scale_ref, *refs):
    col_refs = refs[:col_n]
    out_ref, b_ref, codes_ref, tile_ref, sems = refs[col_n:]
    home_rows = col_refs[0].shape[0]
    tail = segments - lanes
    meta = meta_lane(segments)
    columns = col_n * home_rows
    unit = 1.0 / (16384.0 * full * math.sqrt(segments))
    spans = []
    for k in range(col_n):
        spans.append(pl.multiple_of(place_ref[1, k] * home_rows, home_rows))
        codes_ref[pl.ds(spans[k], home_rows), :] = wide(col_refs[k], main_width, lanes)
    pick = iota((8, lanes), 0)
    chosen = jnp.where((iota((8, lanes), 1) == meta + pick) & (pick < 2 * bins), 1.0, 0.0).astype(jnp.bfloat16)
    high, low = split(codes_ref[...])
    codes = dot_t(chosen, high) + dot_t(chosen, low)

    copies = []
    for f in range(bins):
        slot = f % 2
        for k in range(col_n):
            last = wide(col_refs[k], main_width, lanes)
            high, low = split(wide(col_refs[k], 2 * f * lanes, 2 * lanes))
            mine = ends_of(last, f, tail)
            lane = iota(mine.shape, 1)
            turned = jnp.where(lane < tail, -roll(mine, -tail), roll(mine, tail))
            turned = jnp.where(lane < 2 * tail, turned, 0.0)
            tail_high, tail_low = split(mine)
            ending = line_up(tail_high, tail_high, tail_low, tail)
            b_ref[slot, pl.ds(spans[k], home_rows), :] = jnp.concatenate([high, high, low, ending], axis=1)
            high = jnp.concatenate([-high[:, lanes:], high[:, :lanes]], axis=1)
            low = jnp.concatenate([-low[:, lanes:], low[:, :lanes]], axis=1)
            tail_high, tail_low = split(turned)
            ending = line_up(tail_high, tail_high, tail_low, tail)
            b_ref[slot, pl.ds(columns + spans[k], home_rows), :] = jnp.concatenate([high, high, low, ending], axis=1)
        column_scale = codes[f : f + 1] * jnp.exp2(codes[bins + f : bins + f + 1]) * unit
        row_scale = scale_ref[:, meta + f : meta + f + 1]
        product = dot_t(a_ref[f], b_ref[slot])
        for p in range(2):
            value = product[:, p * columns : (p + 1) * columns] * row_scale * column_scale
            tile_ref[f, p] = value.astype(jnp.bfloat16)
        copies.append(pltpu.make_async_copy(tile_ref.at[f], out_ref.at[f], sems.at[f]))
        copies[f].start()
    for copy in copies:
        copy.wait()


def prepare_rows(place, row_blocks, segments):
    row_n = len(row_blocks)
    rows = row_n * row_blocks[0].shape[0]
    vmem = pl.BlockSpec(memory_space=pltpu.VMEM)
    return pl.pallas_call(
        functools.partial(rows_kernel, segments, row_n),
        out_shape=(
            jax.ShapeDtypeStruct((bins, rows, width), jnp.bfloat16),
            jax.ShapeDtypeStruct((rows, lanes), jnp.float32),
        ),
        in_specs=[pl.BlockSpec(memory_space=pltpu.SMEM)] + [vmem] * row_n,
        out_specs=(vmem, vmem),
        compiler_params=pltpu.CompilerParams(vmem_limit_bytes=vmem_bytes),
        cost_estimate=pl.CostEstimate(flops=1, bytes_accessed=1, transcendentals=0),
        name="prepare_rows",
    )(place, *row_blocks)


def pair_tiles(place, row_parts, row_scales, col_blocks, segments):
    col_n = len(col_blocks)
    rows = row_scales.shape[0]
    columns = col_n * col_blocks[0].shape[0]
    vmem = pl.BlockSpec(memory_space=pltpu.VMEM)
    return pl.pallas_call(
        functools.partial(pair_kernel, segments, col_n),
        in_specs=[pl.BlockSpec(memory_space=pltpu.SMEM)] + [vmem] * (2 + col_n),
        out_specs=pl.BlockSpec(memory_space=pl.ANY),
        scratch_shapes=[
            pltpu.VMEM((2, 2 * columns, width), jnp.bfloat16),
            pltpu.VMEM((columns, lanes), jnp.float32),
            pltpu.VMEM((bins, 2, rows, columns), jnp.bfloat16),
            pltpu.SemaphoreType.DMA((bins,)),
        ],
        out_shape=jax.ShapeDtypeStruct((bins, 2, rows, columns), jnp.bfloat16),
        compiler_params=pltpu.CompilerParams(vmem_limit_bytes=vmem_bytes),
        name="pair_tiles",
    )(place, row_parts, row_scales, *col_blocks)


def copy_kernel(in_ref, out_ref):
    out_ref[...] = in_ref[...]


def copy_block(block, weight):
    vmem = pl.BlockSpec(memory_space=pltpu.VMEM)
    if weight == 0:
        return block
    return pl.pallas_call(
        copy_kernel,
        out_shape=jax.ShapeDtypeStruct(block.shape, block.dtype),
        in_specs=[vmem],
        out_specs=vmem,
        compiler_params=pltpu.CompilerParams(vmem_limit_bytes=vmem_bytes),
        cost_estimate=pl.CostEstimate(flops=weight * 2 * 10**9, bytes_accessed=10**5, transcendentals=0),
        name="copy_block",
    )(block)


def across(value, axis, distance):
    size = lax.axis_size(axis)
    return lax.ppermute(value, axis, [(i, i ^ distance) for i in range(size)])


def gather_columns(white, count):
    blocks = {0: white}
    distance = count // 2
    while distance:
        for k in list(blocks):
            blocks[k + distance] = across(copy_block(blocks[k], 1) if k and distance == 1 else blocks[k], "row", distance)
        distance //= 2
    return [blocks[k] for k in range(count)]


def gather_rows(white, count):
    blocks = {0: white}
    distance = 2
    while distance < count:
        for k in range(0, distance, 2):
            blocks[k + distance] = across(blocks[k], "col", distance)
        distance *= 2
    for k in range(0, count, 2):
        blocks[k + 1] = across(blocks[k], "col", 1)
    return [blocks[k] for k in range(count)]


def shards(spectra, station_ids, counts):
    row_count = lax.axis_size("row")
    column_count = lax.axis_size("col")
    readers = row_count * column_count
    slot_count, segments, _ = spectra.shape
    home_rows = slot_count // 2
    packed = whiten_pack(spectra, station_ids, counts, readers)
    received = lax.all_to_all(packed, ("row", "col"), split_axis=0, concat_axis=0, tiled=True)
    white = settle(received, home_rows, segments)
    row_blocks = gather_rows(white, column_count)
    col_blocks = gather_columns(white, row_count)
    most = jnp.arange(max(row_count, column_count), dtype=jnp.int32)
    place = jnp.stack([lax.axis_index("col") ^ most, lax.axis_index("row") ^ most])
    row_parts, row_scales = prepare_rows(place, row_blocks, segments)
    return pair_tiles(place, row_parts, row_scales, col_blocks, segments)


def solution(mesh):
    in_specs = (P(("row", "col"), None, None), P(("row", "col")), P(("row", "col")))
    out_specs = P(None, None, "row", "col")
    return jax.shard_map(shards, mesh=mesh, in_specs=in_specs, out_specs=out_specs, check_vma=False)
```

```python
import functools
import math

import jax
import jax.numpy as jnp
from jax import lax
from jax.experimental import pallas as pl
from jax.experimental.pallas import tpu as pltpu
from jax.sharding import PartitionSpec as P

power_floor = 0.25
bins = 3
lanes = 128
group = 8
slab = 8
full = 32767.0
vmem_bytes = 48 * 1024 * 1024

tail_tile = 2 * bins
main_width = tail_tile * lanes
width = (tail_tile + 1) * lanes


def meta_lane(segments):
    return tail_tile * (segments - lanes)


def dot_t(a, b):
    return lax.dot_general(a, b, (((1,), (1,)), ((), ())), preferred_element_type=jnp.float32)


def split(q):
    high = q.astype(jnp.bfloat16)
    return high, (q - high.astype(jnp.float32)).astype(jnp.bfloat16)


def iota(shape, dim):
    return lax.broadcasted_iota(jnp.int32, shape, dim)


def roll(x, shift):
    return pltpu.roll(x, shift % x.shape[1], 1)


def whiten_kernel(home_rows, row_count, column_count, parts, count_ref, ids_ref, source_ref, out_ref, x_ref, weight_ref, id_ref, coded_ref, found_ref, stage_ref, ends_ref, sems):
    slot_count, segments, two_band = x_ref.shape
    edges = [slot_count * e // parts[-1] for e in parts]
    copies = []
    for c in range(len(parts) - 1):
        span = pl.ds(edges[c], edges[c + 1] - edges[c])
        copies.append(pltpu.make_async_copy(source_ref.at[span], x_ref.at[span], sems.at[c]))
        copies[c].start()
    band = two_band // 2
    tail = segments - lanes
    depth = group * two_band

    row = iota((lanes, depth), 0)
    col = iota((lanes, depth), 1)
    part = row // group
    same = (row % group) == (col // two_band)
    lane = col % two_band
    lower = (part // 2) * (band // 4)
    center = (part % 2) * band + lower + band // 4
    picks = same & (part < 2 * bins) & (lane == center)
    weight_ref[:, :depth] = jnp.where(picks, 1.0, 0.0).astype(jnp.bfloat16)
    half = depth // 2
    row = iota((lanes, half), 0)
    col = iota((lanes, half), 1)
    part = row // group
    lower = (part - 2 * bins) * (band // 4)
    within = col % band
    inside = (row % group == col // band) & (part >= 2 * bins) & (part < 3 * bins)
    inside = inside & (within >= lower) & (within < lower + band // 2)
    window = jnp.where(inside, 1.0, 0.0).astype(jnp.bfloat16)
    weight_ref[:, depth : depth + half] = window
    weight_ref[:, depth + half :] = window
    left = iota((segments, two_band), 1) < band
    ids = ids_ref[...].astype(jnp.float32)
    local = ids - home_rows * jnp.floor((ids + 0.5) * (1.0 / home_rows))
    eye = iota((slot_count, slot_count), 0) == iota((slot_count, slot_count), 1)
    id_ref[...] = jnp.sum(jnp.where(eye, local + 1.0, 0.0), axis=1, keepdims=True)

    target = jnp.floor((ids + 0.5) * (1.0 / home_rows))
    shape = (slot_count, slot_count)
    j = iota(shape, 0)
    i = iota(shape, 1)
    target_column = jnp.sum(jnp.where(j == i, target, 0.0), axis=1, keepdims=True)
    count = count_ref[0]
    ahead = (j < i) & (j < count) & (target_column == target)
    within = jnp.sum(jnp.where(ahead, 1.0, 0.0), axis=0, keepdims=True)
    live = iota((1, slot_count), 1) < count
    row_of = jnp.floor((target + 0.5) * (1.0 / column_count))
    column_of = target - row_of * column_count
    half_of = jnp.floor((column_of + 0.5) * 0.5)
    core_of = column_of - 2.0 * half_of
    peer = (core_of * (column_count // 2) + half_of) * row_count + row_of
    place = jnp.where(live, peer * slab + within, -1.0)
    send_rows = out_ref.shape[0]
    spot = iota((send_rows, slot_count), 0).astype(jnp.float32)
    chosen = jnp.where(spot == place, 1.0, 0.0).astype(jnp.bfloat16)

    for c in range(len(parts) - 1):
        copies[c].wait()
        for start in range(edges[c], edges[c + 1], group):
            x = x_ref[start : start + group]
            xs = jnp.concatenate([x[s] for s in range(group)], axis=1)
            folded = []
            for s in range(0, group, 2):
                first = x[s]
                second = x[s + 1]
                near = jnp.concatenate([first[:, :band], second[:, band:]], axis=1).astype(jnp.float32)
                far = jnp.concatenate([first[:, band:], second[:, :band]], axis=1).astype(jnp.float32)
                folded.append(near * near + far * far)
            folded = jnp.concatenate(folded, axis=1)
            high = folded.astype(jnp.bfloat16)
            low = (folded - high.astype(jnp.float32)).astype(jnp.bfloat16)
            got = dot_t(jnp.concatenate([xs, high, low], axis=1), weight_ref[...]).T
            for t in range(3 * bins):
                found_ref[t, start : start + group] = got[t * group : (t + 1) * group]

    halves = 2
    for half in range(halves):
        span = slice(half * slot_count // halves, (half + 1) * slot_count // halves)
        last = []
        mants = []
        expos = []
        for f in range(bins):
            gain = lax.rsqrt(jnp.maximum(found_ref[2 * bins + f, span] * (2.0 / band), power_floor))
            pair = [found_ref[2 * f, span] * gain, found_ref[2 * f + 1, span] * gain]
            size = jnp.maximum(jnp.abs(pair[0]), jnp.abs(pair[1]))
            peak = jnp.maximum(jnp.max(size, axis=1, keepdims=True), 1e-30)
            expo = jnp.ceil(jnp.log2(peak))
            mant = jnp.floor(peak * jnp.exp2(-expo) * 16384.0) + 1.0
            inverse = (full * 16384.0) / (mant * jnp.exp2(expo))
            expos.append(expo)
            mants.append(mant)
            for p in range(2):
                q = jnp.clip(jnp.round(pair[p] * inverse), -full, full)
                t = 2 * f + p
                coded_ref[span, t * lanes : (t + 1) * lanes] = q[:, :lanes]
                last.append(q[:, lanes:])
        last += mants + expos + [id_ref[span, :]]
        used = tail_tile * tail + 2 * bins + 1
        last.append(jnp.zeros((slot_count // halves, lanes - used), jnp.float32))
        coded_ref[span, tail_tile * lanes :] = jnp.concatenate(last, axis=1)

    high, low = split(coded_ref[...])
    sent = jnp.dot(chosen, high, preferred_element_type=jnp.float32)
    sent += jnp.dot(chosen, low, preferred_element_type=jnp.float32)
    for t in range(tail_tile):
        stage_ref[t] = sent[:, t * lanes : (t + 1) * lanes]
    ends_ref[...] = sent[:, main_width:]
    readers = send_rows // slab
    for j in range(tail_tile):
        from_rows = ends_ref[pl.ds(j, readers, stride=slab), :]
        stage_ref[j, pl.ds(tail_tile, readers, stride=slab), :] = from_rows
    for t in range(tail_tile):
        out_ref[:, t * lanes : (t + 1) * lanes] = stage_ref[t].astype(jnp.int32).astype(jnp.int16)


def whiten_pack(spectra, station_ids, counts, row_count, column_count):
    readers = row_count * column_count
    slot_count, segments, two_band = spectra.shape
    home_rows = slot_count // 2
    parts = (0, 1, 3)
    return pl.pallas_call(
        functools.partial(whiten_kernel, home_rows, row_count, column_count, parts),
        out_shape=jax.ShapeDtypeStruct((readers * slab, main_width), jnp.int16),
        in_specs=[
            pl.BlockSpec(memory_space=pltpu.SMEM),
            pl.BlockSpec(memory_space=pltpu.VMEM),
            pl.BlockSpec(memory_space=pl.ANY),
        ],
        out_specs=pl.BlockSpec(memory_space=pltpu.VMEM),
        scratch_shapes=[
            pltpu.VMEM(spectra.shape, spectra.dtype),
            pltpu.VMEM((lanes, 2 * group * two_band), jnp.bfloat16),
            pltpu.VMEM((slot_count, 1), jnp.float32),
            pltpu.VMEM((slot_count, width), jnp.float32),
            pltpu.VMEM((3 * bins, slot_count, segments), jnp.float32),
            pltpu.VMEM((tail_tile, readers * slab, lanes), jnp.float32),
            pltpu.VMEM((readers * slab, lanes), jnp.float32),
            pltpu.SemaphoreType.DMA((len(parts) - 1,)),
        ],
        compiler_params=pltpu.CompilerParams(vmem_limit_bytes=vmem_bytes),
        name="whiten_pack",
    )(counts, station_ids.reshape(1, slot_count), spectra)


def settle_kernel(id_lane, in_ref, out_ref, stage_ref, ends_ref):
    home_rows = out_ref.shape[0]
    rows = in_ref.shape[0]
    readers = rows // slab
    for t in range(tail_tile):
        stage_ref[t] = in_ref[:, t * lanes : (t + 1) * lanes].astype(jnp.int32).astype(jnp.float32)
    ends_ref[...] = jnp.zeros_like(ends_ref)
    for j in range(tail_tile):
        from_rows = stage_ref[j, pl.ds(tail_tile, readers, stride=slab), :]
        ends_ref[pl.ds(j, readers, stride=slab), :] = from_rows
    ends = ends_ref[...]
    station = ends[:, id_lane : id_lane + 1]
    wanted = (iota((rows, home_rows), 1) + 1).astype(jnp.float32)
    chosen = jnp.where(station == wanted, 1.0, 0.0).astype(jnp.bfloat16)
    dims = (((0,), (0,)), ((), ()))
    high, low = split(jnp.concatenate([stage_ref[t] for t in range(tail_tile)] + [ends], axis=1))
    home = lax.dot_general(chosen, high, dims, preferred_element_type=jnp.float32)
    home += lax.dot_general(chosen, low, dims, preferred_element_type=jnp.float32)
    out_ref[...] = home.astype(jnp.int32).astype(jnp.int16)


def settle(received, home_rows, segments):
    return pl.pallas_call(
        functools.partial(settle_kernel, meta_lane(segments) + 2 * bins),
        out_shape=jax.ShapeDtypeStruct((home_rows, width), jnp.int16),
        scratch_shapes=[
            pltpu.VMEM((tail_tile, received.shape[0], lanes), jnp.float32),
            pltpu.VMEM((received.shape[0], lanes), jnp.float32),
        ],
        compiler_params=pltpu.CompilerParams(vmem_limit_bytes=vmem_bytes),
        name="settle",
    )(received)


def ends_of(last, f, tail):
    mine = last if f == 0 else roll(last, -f * 2 * tail)
    return jnp.where(iota(mine.shape, 1) < 2 * tail, mine, 0.0)


def line_up(first, second, third, tail):
    ending = first.astype(jnp.float32) + roll(second.astype(jnp.float32), 2 * tail)
    return (ending + roll(third.astype(jnp.float32), 4 * tail)).astype(jnp.bfloat16)


def wide(ref, start, size):
    return ref[:, start : start + size].astype(jnp.int32).astype(jnp.float32)


def rows_kernel(segments, row_n, place_ref, *refs):
    row_refs = refs[:row_n]
    a_ref, scale_ref = refs[row_n:]
    home_rows = row_refs[0].shape[0]
    tail = segments - lanes
    for k in range(row_n):
        start = pl.multiple_of(place_ref[0, k] * home_rows, home_rows)
        span = pl.ds(start, home_rows)
        last = wide(row_refs[k], main_width, lanes)
        scale_ref[span, :] = last * jnp.exp2(roll(last, -bins)) * (1.0 / (16384.0 * full))
        for f in range(bins):
            high, low = split(wide(row_refs[k], 2 * f * lanes, 2 * lanes))
            tail_high, tail_low = split(ends_of(last, f, tail))
            ending = line_up(tail_high, tail_low, tail_high, tail)
            a_ref[f, span, :] = jnp.concatenate([high, low, high, ending], axis=1)


def pair_kernel(segments, col_n, place_ref, a_ref, scale_ref, *refs):
    col_refs = refs[:col_n]
    out_ref, b_ref, codes_ref, tile_ref, sems = refs[col_n:]
    home_rows = col_refs[0].shape[0]
    tail = segments - lanes
    meta = meta_lane(segments)
    columns = col_n * home_rows
    unit = 1.0 / (16384.0 * full * math.sqrt(segments))
    spans = []
    for k in range(col_n):
        spans.append(pl.multiple_of(place_ref[1, k] * home_rows, home_rows))
        codes_ref[pl.ds(spans[k], home_rows), :] = wide(col_refs[k], main_width, lanes)
    pick = iota((8, lanes), 0)
    chosen = jnp.where((iota((8, lanes), 1) == meta + pick) & (pick < 2 * bins), 1.0, 0.0).astype(jnp.bfloat16)
    high, low = split(codes_ref[...])
    codes = dot_t(chosen, high) + dot_t(chosen, low)

    copies = []
    for f in range(bins):
        slot = f % 2
        for k in range(col_n):
            last = wide(col_refs[k], main_width, lanes)
            high, low = split(wide(col_refs[k], 2 * f * lanes, 2 * lanes))
            mine = ends_of(last, f, tail)
            lane = iota(mine.shape, 1)
            turned = jnp.where(lane < tail, -roll(mine, -tail), roll(mine, tail))
            turned = jnp.where(lane < 2 * tail, turned, 0.0)
            tail_high, tail_low = split(mine)
            ending = line_up(tail_high, tail_high, tail_low, tail)
            b_ref[slot, pl.ds(spans[k], home_rows), :] = jnp.concatenate([high, high, low, ending], axis=1)
            high = jnp.concatenate([-high[:, lanes:], high[:, :lanes]], axis=1)
            low = jnp.concatenate([-low[:, lanes:], low[:, :lanes]], axis=1)
            tail_high, tail_low = split(turned)
            ending = line_up(tail_high, tail_high, tail_low, tail)
            b_ref[slot, pl.ds(columns + spans[k], home_rows), :] = jnp.concatenate([high, high, low, ending], axis=1)
        column_scale = codes[f : f + 1] * jnp.exp2(codes[bins + f : bins + f + 1]) * unit
        row_scale = scale_ref[:, meta + f : meta + f + 1]
        product = dot_t(a_ref[f], b_ref[slot])
        for p in range(2):
            value = product[:, p * columns : (p + 1) * columns] * row_scale * column_scale
            tile_ref[f, p] = value.astype(jnp.bfloat16)
        copies.append(pltpu.make_async_copy(tile_ref.at[f], out_ref.at[f], sems.at[f]))
        copies[f].start()
    for copy in copies:
        copy.wait()


def prepare_rows(place, row_blocks, segments):
    row_n = len(row_blocks)
    rows = row_n * row_blocks[0].shape[0]
    vmem = pl.BlockSpec(memory_space=pltpu.VMEM)
    return pl.pallas_call(
        functools.partial(rows_kernel, segments, row_n),
        out_shape=(
            jax.ShapeDtypeStruct((bins, rows, width), jnp.bfloat16),
            jax.ShapeDtypeStruct((rows, lanes), jnp.float32),
        ),
        in_specs=[pl.BlockSpec(memory_space=pltpu.SMEM)] + [vmem] * row_n,
        out_specs=(vmem, vmem),
        compiler_params=pltpu.CompilerParams(vmem_limit_bytes=vmem_bytes),
        cost_estimate=pl.CostEstimate(flops=1, bytes_accessed=1, transcendentals=0),
        name="prepare_rows",
    )(place, *row_blocks)


def pair_tiles(place, row_parts, row_scales, col_blocks, segments):
    col_n = len(col_blocks)
    rows = row_scales.shape[0]
    columns = col_n * col_blocks[0].shape[0]
    vmem = pl.BlockSpec(memory_space=pltpu.VMEM)
    return pl.pallas_call(
        functools.partial(pair_kernel, segments, col_n),
        in_specs=[pl.BlockSpec(memory_space=pltpu.SMEM)] + [vmem] * (2 + col_n),
        out_specs=pl.BlockSpec(memory_space=pl.ANY),
        scratch_shapes=[
            pltpu.VMEM((2, 2 * columns, width), jnp.bfloat16),
            pltpu.VMEM((columns, lanes), jnp.float32),
            pltpu.VMEM((bins, 2, rows, columns), jnp.bfloat16),
            pltpu.SemaphoreType.DMA((bins,)),
        ],
        out_shape=jax.ShapeDtypeStruct((bins, 2, rows, columns), jnp.bfloat16),
        compiler_params=pltpu.CompilerParams(vmem_limit_bytes=vmem_bytes),
        name="pair_tiles",
    )(place, row_parts, row_scales, *col_blocks)


def copy_kernel(in_ref, out_ref):
    out_ref[...] = in_ref[...]


def copy_block(block, weight):
    vmem = pl.BlockSpec(memory_space=pltpu.VMEM)
    if weight == 0:
        return block
    return pl.pallas_call(
        copy_kernel,
        out_shape=jax.ShapeDtypeStruct(block.shape, block.dtype),
        in_specs=[vmem],
        out_specs=vmem,
        compiler_params=pltpu.CompilerParams(vmem_limit_bytes=vmem_bytes),
        cost_estimate=pl.CostEstimate(flops=weight * 2 * 10**9, bytes_accessed=10**5, transcendentals=0),
        name="copy_block",
    )(block)


def across(value, axis, distance):
    size = lax.axis_size(axis)
    return lax.ppermute(value, axis, [(i, i ^ distance) for i in range(size)])


def gather_columns(white, count):
    blocks = {0: white}
    distance = count // 2
    while distance:
        for k in list(blocks):
            blocks[k + distance] = across(copy_block(blocks[k], 1) if k and distance == 1 else blocks[k], "row", distance)
        distance //= 2
    return [blocks[k] for k in range(count)]


def gather_rows(white, count):
    blocks = {0: white}
    distance = 2
    while distance < count:
        for k in range(0, distance, 2):
            blocks[k + distance] = across(blocks[k], "col", distance)
        distance *= 2
    for k in range(0, count, 2):
        blocks[k + 1] = across(blocks[k], "col", 1)
    return [blocks[k] for k in range(count)]


def shards(spectra, station_ids, counts):
    row_count = lax.axis_size("row")
    column_count = lax.axis_size("col")
    slot_count, segments, _ = spectra.shape
    home_rows = slot_count // 2
    packed = whiten_pack(spectra, station_ids, counts, row_count, column_count)
    order = [r * column_count + 2 * h + k for k in range(2) for h in range(column_count // 2) for r in range(row_count)]
    received = lax.all_to_all(
        packed, ("row", "col"), split_axis=0, concat_axis=0, tiled=True, axis_index_groups=[order]
    )
    white = settle(received, home_rows, segments)
    row_blocks = gather_rows(white, column_count)
    col_blocks = gather_columns(white, row_count)
    most = jnp.arange(max(row_count, column_count), dtype=jnp.int32)
    place = jnp.stack([lax.axis_index("col") ^ most, lax.axis_index("row") ^ most])
    row_parts, row_scales = prepare_rows(place, row_blocks, segments)
    return pair_tiles(place, row_parts, row_scales, col_blocks, segments)


def solution(mesh):
    in_specs = (P(("row", "col"), None, None), P(("row", "col")), P(("row", "col")))
    out_specs = P(None, None, "row", "col")
    return jax.shard_map(shards, mesh=mesh, in_specs=in_specs, out_specs=out_specs, check_vma=False)
```

```python
import functools
import math

import jax
import jax.numpy as jnp
from jax import lax
from jax.experimental import pallas as pl
from jax.experimental.pallas import tpu as pltpu
from jax.sharding import PartitionSpec as P

power_floor = 0.25
bins = 3
lanes = 128
group = 8
slab = 8
full = 32767.0
vmem_bytes = 48 * 1024 * 1024

tail_tile = 2 * bins
main_width = tail_tile * lanes
width = (tail_tile + 1) * lanes


def meta_lane(segments):
    return tail_tile * (segments - lanes)


def dot_t(a, b):
    return lax.dot_general(a, b, (((1,), (1,)), ((), ())), preferred_element_type=jnp.float32)


def split(q):
    high = q.astype(jnp.bfloat16)
    return high, (q - high.astype(jnp.float32)).astype(jnp.bfloat16)


def iota(shape, dim):
    return lax.broadcasted_iota(jnp.int32, shape, dim)


def roll(x, shift):
    return pltpu.roll(x, shift % x.shape[1], 1)


def whiten_kernel(home_rows, row_count, column_count, parts, count_ref, ids_ref, source_ref, out_ref, x_ref, weight_ref, id_ref, coded_ref, found_ref, stage_ref, ends_ref, sems):
    slot_count, segments, two_band = x_ref.shape
    edges = [slot_count * e // parts[-1] for e in parts]
    copies = []
    for c in range(len(parts) - 1):
        span = pl.ds(edges[c], edges[c + 1] - edges[c])
        copies.append(pltpu.make_async_copy(source_ref.at[span], x_ref.at[span], sems.at[c]))
        copies[c].start()
    band = two_band // 2
    tail = segments - lanes
    depth = group * two_band

    row = iota((lanes, depth), 0)
    col = iota((lanes, depth), 1)
    part = row // group
    same = (row % group) == (col // two_band)
    lane = col % two_band
    lower = (part // 2) * (band // 4)
    center = (part % 2) * band + lower + band // 4
    picks = same & (part < 2 * bins) & (lane == center)
    weight_ref[:, :depth] = jnp.where(picks, 1.0, 0.0).astype(jnp.bfloat16)
    half = depth // 2
    row = iota((lanes, half), 0)
    col = iota((lanes, half), 1)
    part = row // group
    lower = (part - 2 * bins) * (band // 4)
    within = col % band
    inside = (row % group == col // band) & (part >= 2 * bins) & (part < 3 * bins)
    inside = inside & (within >= lower) & (within < lower + band // 2)
    window = jnp.where(inside, 1.0, 0.0).astype(jnp.bfloat16)
    weight_ref[:, depth : depth + half] = window
    weight_ref[:, depth + half :] = window
    left = iota((segments, two_band), 1) < band
    ids = ids_ref[...].astype(jnp.float32)
    local = ids - home_rows * jnp.floor((ids + 0.5) * (1.0 / home_rows))
    eye = iota((slot_count, slot_count), 0) == iota((slot_count, slot_count), 1)
    id_ref[...] = jnp.sum(jnp.where(eye, local + 1.0, 0.0), axis=1, keepdims=True)

    target = jnp.floor((ids + 0.5) * (1.0 / home_rows))
    shape = (slot_count, slot_count)
    j = iota(shape, 0)
    i = iota(shape, 1)
    target_column = jnp.sum(jnp.where(j == i, target, 0.0), axis=1, keepdims=True)
    count = count_ref[0]
    ahead = (j < i) & (j < count) & (target_column == target)
    within = jnp.sum(jnp.where(ahead, 1.0, 0.0), axis=0, keepdims=True)
    live = iota((1, slot_count), 1) < count
    row_of = jnp.floor((target + 0.5) * (1.0 / column_count))
    column_of = target - row_of * column_count
    half_of = jnp.floor((column_of + 0.5) * 0.5)
    core_of = column_of - 2.0 * half_of
    peer = (core_of * row_count + row_of) * (column_count // 2) + half_of
    place = jnp.where(live, peer * slab + within, -1.0)
    send_rows = out_ref.shape[0]
    spot = iota((send_rows, slot_count), 0).astype(jnp.float32)
    chosen = jnp.where(spot == place, 1.0, 0.0).astype(jnp.bfloat16)

    for c in range(len(parts) - 1):
        copies[c].wait()
        for start in range(edges[c], edges[c + 1], group):
            x = x_ref[start : start + group]
            xs = jnp.concatenate([x[s] for s in range(group)], axis=1)
            folded = []
            for s in range(0, group, 2):
                first = x[s]
                second = x[s + 1]
                near = jnp.concatenate([first[:, :band], second[:, band:]], axis=1).astype(jnp.float32)
                far = jnp.concatenate([first[:, band:], second[:, :band]], axis=1).astype(jnp.float32)
                folded.append(near * near + far * far)
            folded = jnp.concatenate(folded, axis=1)
            high = folded.astype(jnp.bfloat16)
            low = (folded - high.astype(jnp.float32)).astype(jnp.bfloat16)
            got = dot_t(jnp.concatenate([xs, high, low], axis=1), weight_ref[...]).T
            for t in range(3 * bins):
                found_ref[t, start : start + group] = got[t * group : (t + 1) * group]

    halves = 2
    for half in range(halves):
        span = slice(half * slot_count // halves, (half + 1) * slot_count // halves)
        last = []
        mants = []
        expos = []
        for f in range(bins):
            gain = lax.rsqrt(jnp.maximum(found_ref[2 * bins + f, span] * (2.0 / band), power_floor))
            pair = [found_ref[2 * f, span] * gain, found_ref[2 * f + 1, span] * gain]
            size = jnp.maximum(jnp.abs(pair[0]), jnp.abs(pair[1]))
            peak = jnp.maximum(jnp.max(size, axis=1, keepdims=True), 1e-30)
            expo = jnp.ceil(jnp.log2(peak))
            mant = jnp.floor(peak * jnp.exp2(-expo) * 16384.0) + 1.0
            inverse = (full * 16384.0) / (mant * jnp.exp2(expo))
            expos.append(expo)
            mants.append(mant)
            for p in range(2):
                q = jnp.clip(jnp.round(pair[p] * inverse), -full, full)
                t = 2 * f + p
                coded_ref[span, t * lanes : (t + 1) * lanes] = q[:, :lanes]
                last.append(q[:, lanes:])
        last += mants + expos + [id_ref[span, :]]
        used = tail_tile * tail + 2 * bins + 1
        last.append(jnp.zeros((slot_count // halves, lanes - used), jnp.float32))
        coded_ref[span, tail_tile * lanes :] = jnp.concatenate(last, axis=1)

    high, low = split(coded_ref[...])
    sent = jnp.dot(chosen, high, preferred_element_type=jnp.float32)
    sent += jnp.dot(chosen, low, preferred_element_type=jnp.float32)
    for t in range(tail_tile):
        stage_ref[t] = sent[:, t * lanes : (t + 1) * lanes]
    ends_ref[...] = sent[:, main_width:]
    readers = send_rows // slab
    for j in range(tail_tile):
        from_rows = ends_ref[pl.ds(j, readers, stride=slab), :]
        stage_ref[j, pl.ds(tail_tile, readers, stride=slab), :] = from_rows
    for t in range(tail_tile):
        out_ref[:, t * lanes : (t + 1) * lanes] = stage_ref[t].astype(jnp.int32).astype(jnp.int16)


def whiten_pack(spectra, station_ids, counts, row_count, column_count):
    readers = row_count * column_count
    slot_count, segments, two_band = spectra.shape
    home_rows = slot_count // 2
    parts = (0, 1, 3)
    return pl.pallas_call(
        functools.partial(whiten_kernel, home_rows, row_count, column_count, parts),
        out_shape=jax.ShapeDtypeStruct((readers * slab, main_width), jnp.int16),
        in_specs=[
            pl.BlockSpec(memory_space=pltpu.SMEM),
            pl.BlockSpec(memory_space=pltpu.VMEM),
            pl.BlockSpec(memory_space=pl.ANY),
        ],
        out_specs=pl.BlockSpec(memory_space=pltpu.VMEM),
        scratch_shapes=[
            pltpu.VMEM(spectra.shape, spectra.dtype),
            pltpu.VMEM((lanes, 2 * group * two_band), jnp.bfloat16),
            pltpu.VMEM((slot_count, 1), jnp.float32),
            pltpu.VMEM((slot_count, width), jnp.float32),
            pltpu.VMEM((3 * bins, slot_count, segments), jnp.float32),
            pltpu.VMEM((tail_tile, readers * slab, lanes), jnp.float32),
            pltpu.VMEM((readers * slab, lanes), jnp.float32),
            pltpu.SemaphoreType.DMA((len(parts) - 1,)),
        ],
        compiler_params=pltpu.CompilerParams(vmem_limit_bytes=vmem_bytes),
        name="whiten_pack",
    )(counts, station_ids.reshape(1, slot_count), spectra)


def settle_kernel(id_lane, in_ref, out_ref, stage_ref, ends_ref):
    home_rows = out_ref.shape[0]
    rows = in_ref.shape[0]
    readers = rows // slab
    for t in range(tail_tile):
        stage_ref[t] = in_ref[:, t * lanes : (t + 1) * lanes].astype(jnp.int32).astype(jnp.float32)
    ends_ref[...] = jnp.zeros_like(ends_ref)
    for j in range(tail_tile):
        from_rows = stage_ref[j, pl.ds(tail_tile, readers, stride=slab), :]
        ends_ref[pl.ds(j, readers, stride=slab), :] = from_rows
    ends = ends_ref[...]
    station = ends[:, id_lane : id_lane + 1]
    wanted = (iota((rows, home_rows), 1) + 1).astype(jnp.float32)
    chosen = jnp.where(station == wanted, 1.0, 0.0).astype(jnp.bfloat16)
    dims = (((0,), (0,)), ((), ()))
    high, low = split(jnp.concatenate([stage_ref[t] for t in range(tail_tile)] + [ends], axis=1))
    home = lax.dot_general(chosen, high, dims, preferred_element_type=jnp.float32)
    home += lax.dot_general(chosen, low, dims, preferred_element_type=jnp.float32)
    out_ref[...] = home.astype(jnp.int32).astype(jnp.int16)


def settle(received, home_rows, segments):
    return pl.pallas_call(
        functools.partial(settle_kernel, meta_lane(segments) + 2 * bins),
        out_shape=jax.ShapeDtypeStruct((home_rows, width), jnp.int16),
        scratch_shapes=[
            pltpu.VMEM((tail_tile, received.shape[0], lanes), jnp.float32),
            pltpu.VMEM((received.shape[0], lanes), jnp.float32),
        ],
        compiler_params=pltpu.CompilerParams(vmem_limit_bytes=vmem_bytes),
        name="settle",
    )(received)


def ends_of(last, f, tail):
    mine = last if f == 0 else roll(last, -f * 2 * tail)
    return jnp.where(iota(mine.shape, 1) < 2 * tail, mine, 0.0)


def line_up(first, second, third, tail):
    ending = first.astype(jnp.float32) + roll(second.astype(jnp.float32), 2 * tail)
    return (ending + roll(third.astype(jnp.float32), 4 * tail)).astype(jnp.bfloat16)


def wide(ref, start, size):
    return ref[:, start : start + size].astype(jnp.int32).astype(jnp.float32)


def rows_kernel(segments, row_n, place_ref, *refs):
    row_refs = refs[:row_n]
    a_ref, scale_ref = refs[row_n:]
    home_rows = row_refs[0].shape[0]
    tail = segments - lanes
    for k in range(row_n):
        start = pl.multiple_of(place_ref[0, k] * home_rows, home_rows)
        span = pl.ds(start, home_rows)
        last = wide(row_refs[k], main_width, lanes)
        scale_ref[span, :] = last * jnp.exp2(roll(last, -bins)) * (1.0 / (16384.0 * full))
        for f in range(bins):
            high, low = split(wide(row_refs[k], 2 * f * lanes, 2 * lanes))
            tail_high, tail_low = split(ends_of(last, f, tail))
            ending = line_up(tail_high, tail_low, tail_high, tail)
            a_ref[f, span, :] = jnp.concatenate([high, low, high, ending], axis=1)


def pair_kernel(segments, col_n, place_ref, a_ref, scale_ref, *refs):
    col_refs = refs[:col_n]
    out_ref, b_ref, codes_ref, tile_ref, sems = refs[col_n:]
    home_rows = col_refs[0].shape[0]
    tail = segments - lanes
    meta = meta_lane(segments)
    columns = col_n * home_rows
    unit = 1.0 / (16384.0 * full * math.sqrt(segments))
    spans = []
    for k in range(col_n):
        spans.append(pl.multiple_of(place_ref[1, k] * home_rows, home_rows))
        codes_ref[pl.ds(spans[k], home_rows), :] = wide(col_refs[k], main_width, lanes)
    pick = iota((8, lanes), 0)
    chosen = jnp.where((iota((8, lanes), 1) == meta + pick) & (pick < 2 * bins), 1.0, 0.0).astype(jnp.bfloat16)
    high, low = split(codes_ref[...])
    codes = dot_t(chosen, high) + dot_t(chosen, low)

    copies = []
    for f in range(bins):
        slot = f % 2
        for k in range(col_n):
            last = wide(col_refs[k], main_width, lanes)
            high, low = split(wide(col_refs[k], 2 * f * lanes, 2 * lanes))
            mine = ends_of(last, f, tail)
            lane = iota(mine.shape, 1)
            turned = jnp.where(lane < tail, -roll(mine, -tail), roll(mine, tail))
            turned = jnp.where(lane < 2 * tail, turned, 0.0)
            tail_high, tail_low = split(mine)
            ending = line_up(tail_high, tail_high, tail_low, tail)
            b_ref[slot, pl.ds(spans[k], home_rows), :] = jnp.concatenate([high, high, low, ending], axis=1)
            high = jnp.concatenate([-high[:, lanes:], high[:, :lanes]], axis=1)
            low = jnp.concatenate([-low[:, lanes:], low[:, :lanes]], axis=1)
            tail_high, tail_low = split(turned)
            ending = line_up(tail_high, tail_high, tail_low, tail)
            b_ref[slot, pl.ds(columns + spans[k], home_rows), :] = jnp.concatenate([high, high, low, ending], axis=1)
        column_scale = codes[f : f + 1] * jnp.exp2(codes[bins + f : bins + f + 1]) * unit
        row_scale = scale_ref[:, meta + f : meta + f + 1]
        product = dot_t(a_ref[f], b_ref[slot])
        for p in range(2):
            value = product[:, p * columns : (p + 1) * columns] * row_scale * column_scale
            tile_ref[f, p] = value.astype(jnp.bfloat16)
        copies.append(pltpu.make_async_copy(tile_ref.at[f], out_ref.at[f], sems.at[f]))
        copies[f].start()
    for copy in copies:
        copy.wait()


def prepare_rows(place, row_blocks, segments):
    row_n = len(row_blocks)
    rows = row_n * row_blocks[0].shape[0]
    vmem = pl.BlockSpec(memory_space=pltpu.VMEM)
    return pl.pallas_call(
        functools.partial(rows_kernel, segments, row_n),
        out_shape=(
            jax.ShapeDtypeStruct((bins, rows, width), jnp.bfloat16),
            jax.ShapeDtypeStruct((rows, lanes), jnp.float32),
        ),
        in_specs=[pl.BlockSpec(memory_space=pltpu.SMEM)] + [vmem] * row_n,
        out_specs=(vmem, vmem),
        compiler_params=pltpu.CompilerParams(vmem_limit_bytes=vmem_bytes),
        cost_estimate=pl.CostEstimate(flops=1, bytes_accessed=1, transcendentals=0),
        name="prepare_rows",
    )(place, *row_blocks)


def pair_tiles(place, row_parts, row_scales, col_blocks, segments):
    col_n = len(col_blocks)
    rows = row_scales.shape[0]
    columns = col_n * col_blocks[0].shape[0]
    vmem = pl.BlockSpec(memory_space=pltpu.VMEM)
    return pl.pallas_call(
        functools.partial(pair_kernel, segments, col_n),
        in_specs=[pl.BlockSpec(memory_space=pltpu.SMEM)] + [vmem] * (2 + col_n),
        out_specs=pl.BlockSpec(memory_space=pl.ANY),
        scratch_shapes=[
            pltpu.VMEM((2, 2 * columns, width), jnp.bfloat16),
            pltpu.VMEM((columns, lanes), jnp.float32),
            pltpu.VMEM((bins, 2, rows, columns), jnp.bfloat16),
            pltpu.SemaphoreType.DMA((bins,)),
        ],
        out_shape=jax.ShapeDtypeStruct((bins, 2, rows, columns), jnp.bfloat16),
        compiler_params=pltpu.CompilerParams(vmem_limit_bytes=vmem_bytes),
        name="pair_tiles",
    )(place, row_parts, row_scales, *col_blocks)


def copy_kernel(in_ref, out_ref):
    out_ref[...] = in_ref[...]


def copy_block(block, weight):
    vmem = pl.BlockSpec(memory_space=pltpu.VMEM)
    if weight == 0:
        return block
    return pl.pallas_call(
        copy_kernel,
        out_shape=jax.ShapeDtypeStruct(block.shape, block.dtype),
        in_specs=[vmem],
        out_specs=vmem,
        compiler_params=pltpu.CompilerParams(vmem_limit_bytes=vmem_bytes),
        cost_estimate=pl.CostEstimate(flops=weight * 2 * 10**9, bytes_accessed=10**5, transcendentals=0),
        name="copy_block",
    )(block)


def across(value, axis, distance):
    size = lax.axis_size(axis)
    return lax.ppermute(value, axis, [(i, i ^ distance) for i in range(size)])


def gather_columns(white, count):
    blocks = {0: white}
    distance = count // 2
    while distance:
        for k in list(blocks):
            blocks[k + distance] = across(copy_block(blocks[k], 1) if k and distance == 1 else blocks[k], "row", distance)
        distance //= 2
    return [blocks[k] for k in range(count)]


def gather_rows(white, count):
    blocks = {0: white}
    distance = 2
    while distance < count:
        for k in range(0, distance, 2):
            blocks[k + distance] = across(blocks[k], "col", distance)
        distance *= 2
    for k in range(0, count, 2):
        blocks[k + 1] = across(blocks[k], "col", 1)
    return [blocks[k] for k in range(count)]


def shards(spectra, station_ids, counts):
    row_count = lax.axis_size("row")
    column_count = lax.axis_size("col")
    slot_count, segments, _ = spectra.shape
    home_rows = slot_count // 2
    packed = whiten_pack(spectra, station_ids, counts, row_count, column_count)
    order = [r * column_count + 2 * h + k for k in range(2) for r in range(row_count) for h in range(column_count // 2)]
    received = lax.all_to_all(
        packed, ("row", "col"), split_axis=0, concat_axis=0, tiled=True, axis_index_groups=[order]
    )
    white = settle(received, home_rows, segments)
    row_blocks = gather_rows(white, column_count)
    col_blocks = gather_columns(white, row_count)
    most = jnp.arange(max(row_count, column_count), dtype=jnp.int32)
    place = jnp.stack([lax.axis_index("col") ^ most, lax.axis_index("row") ^ most])
    row_parts, row_scales = prepare_rows(place, row_blocks, segments)
    return pair_tiles(place, row_parts, row_scales, col_blocks, segments)


def solution(mesh):
    in_specs = (P(("row", "col"), None, None), P(("row", "col")), P(("row", "col")))
    out_specs = P(None, None, "row", "col")
    return jax.shard_map(shards, mesh=mesh, in_specs=in_specs, out_specs=out_specs, check_vma=False)
```
